32 devices in a mesh: seq: 4 (over y, x), chan: 8 (over z, core).
Axes of the slice: x: 2, y: 2, z: 4, core: 2. Of those that a mesh axis runs over, the one named last changes fastest.
Arguments:
- signal: float32 [2048, 4096], P('seq', 'chan'), may hold values from -6 to 6
- filter_taps: float32 [2048, 4096], P('seq', 'chan'), may hold values from -3 to 3
- out_gate: float32 [2048, 4096], P('seq', 'chan'), may hold values from -6 to 6
- skip_gain: float32 [4096], P('chan'), may hold values from -4 to 4
- lengths: int32 [32], replicated, may hold values from 1 to 512, 2048 in all
- row_of_segment: int32 [32], replicated, may hold values from 0 to 31, each once
Outputs:
- mixed: float32 [2048, 4096], P('seq', 'chan')
- pooled: float32 [32, 4096], P('seq', 'chan')
The draws below stay inside these ranges and needn't reach their ends.
Inputs may be any that keep to these rules, and one draw needn't show every extreme that they name: `lengths`: segments tile the sequence; pooled row r belongs to index r // 8 of seq. `row_of_segment`: each row appears once.
All inputs are finite; a program needn't handle non-finite values.
Results may differ from the reference program's by a relative error of at most 0.000078.
Values sent between devices are 32-bit elements; how exact they have to be, the bound alone decides.
A program may use at most 64 MiB of HBM per device.

```python
import math
import jax
import jax.numpy as jnp
import numpy as np
from jax import lax

D = 4096
TOK_DEV = 512
TOKENS = 2048
SEGS = 32


def draw_filter_taps(key, part):
    key_decay, key_values = jax.random.split(key)
    low_end = math.log(20.0)
    decay_len = jnp.exp(jax.random.uniform(key_decay, (D,), jnp.float32, low_end, math.log(4.0 * TOKENS)))
    noise_part = jnp.clip(jax.random.normal(key_values, (TOKENS, D), jnp.float32), -6.0, 6.0)
    places = jnp.arange(TOKENS, dtype=jnp.float32)[:, None]
    envelope = jnp.exp(-places / decay_len[None, :]) * jnp.sqrt(2.0 / decay_len)[None, :]
    return noise_part * envelope


def block_levels(own_key, dims, cuts, low, high):
    gain, own = 1.0, jax.random.fold_in(own_key, 6)
    for axis_at, blocks in cuts:
        steps = jnp.exp(jax.random.uniform(jax.random.fold_in(own, axis_at), (blocks,), jnp.float32, low / len(cuts), high / len(cuts)))
        gain = gain * jnp.repeat(steps, dims[axis_at] // blocks).reshape([-1 if axis == axis_at else 1 for axis in range(len(dims))])
    return gain


def split_up(amount, total, most, skew):
    portions = [(1 << 20) // math.isqrt(grade ** skew) + 1 for grade in range(2, amount + 1)]
    spare, holding = total - most - (amount - 1), [1] * (amount - 1)
    while spare > 0:
        candidates = [i for i in range(amount - 1) if holding[i] < most]
        whole, remaining = sum([portions[i] for i in candidates]), spare
        for i in candidates:
            more = min(most - holding[i], max(1, remaining * portions[i] // whole), spare)
            holding[i] = holding[i] + more
            spare = spare - more
    return np.array([most] + holding)


def uneven(key, amount, total, reach, lean):
    if amount == 2:
        one = jax.random.randint(key, (), max(1, total - reach), min(reach, total - 1) + 1)
        return jnp.stack([one, total - one])
    sizes = jnp.asarray(split_up(amount, total, reach, lean), jnp.int32)
    pairs = (amount - 1) // 2
    donor, sink = sizes[1:1 + 2 * pairs:2], sizes[2:2 + 2 * pairs:2]
    room = jnp.minimum(donor - 1, reach - sink)
    passed = jax.random.randint(jax.random.fold_in(key, 1), (pairs,), 0, 1 << 20) % (room + 1)
    sizes = sizes.at[1:1 + 2 * pairs:2].set(donor - passed).at[2:2 + 2 * pairs:2].set(sink + passed)
    return sizes[jax.random.permutation(jax.random.fold_in(key, 2), amount)]


def scatter_about(key, shape, deviation, reach, pieces=(), held_as=jnp.bfloat16):
    drawn = deviation * jax.random.normal(key, shape, jnp.float32)
    if pieces:
        drawn = drawn * block_levels(key, shape, pieces, -0.22, 0.18)
    return jnp.clip(drawn, -reach, reach).astype(held_as)


def setup_inputs(seed: int = 0) -> dict:
    key_of = jax.random.split(jax.random.key(seed), 7)
    return {
        "signal": scatter_about(key_of[0], (TOKENS, D), 1.0, 6.0, ((0, 4), (1, 8)), jnp.float32),
        "filter_taps": draw_filter_taps(jax.random.fold_in(key_of[6], 71), 0),
        "out_gate": scatter_about(key_of[2], (TOKENS, D), 1.0, 6.0, ((0, 4), (1, 8)), jnp.float32),
        "skip_gain": scatter_about(key_of[3], (D,), 1.0, 4.0, ((0, 8),), jnp.float32),
        "lengths": uneven(key_of[4], SEGS, TOKENS, TOK_DEV, 2).astype(jnp.int32),
        "row_of_segment": jax.random.permutation(key_of[5], SEGS).astype(jnp.int32),
    }


def convolve_block(pair):
    signal_block, taps_block = pair
    signal_spec = jnp.fft.rfft(signal_block, n=2 * TOKENS, axis=0)
    taps_spec = jnp.fft.rfft(taps_block, n=2 * TOKENS, axis=0)
    return jnp.fft.irfft(signal_spec * taps_spec, n=2 * TOKENS, axis=0)[:TOKENS]


def reference(signal, filter_taps, out_gate, skip_gain, lengths, row_of_segment):
    block_width = min(256, D)
    groups = D // block_width
    signal_blocks = jnp.transpose(signal.reshape(TOKENS, groups, block_width), (1, 0, 2))
    taps_blocks = jnp.transpose(filter_taps.reshape(TOKENS, groups, block_width), (1, 0, 2))
    conv_blocks = lax.map(convolve_block, (signal_blocks, taps_blocks))
    conv = jnp.transpose(conv_blocks, (1, 0, 2)).reshape(TOKENS, D).astype(signal.dtype)
    mixed = out_gate * (conv + skip_gain[None, :] * signal)
    segment_ids = jnp.repeat(jnp.arange(SEGS, dtype=jnp.int32), lengths, total_repeat_length=TOKENS)
    sums = jax.ops.segment_sum(mixed, segment_ids, num_segments=SEGS)
    means = sums / lengths.astype(mixed.dtype)[:, None]
    pooled = jnp.zeros_like(means).at[row_of_segment].set(means)
    return mixed, pooled
```

```python
import functools
import math

import jax
import jax.numpy as jnp
import ml_dtypes
import numpy as np
from jax import lax
from jax.experimental import pallas as pl
from jax.experimental.pallas import tpu as pltpu
from jax.sharding import PartitionSpec as P

LANES = 128
MESH = pl.DeviceIdType.MESH

exact_mode = lax.Precision.HIGHEST


def complex_dot(left_re, left_im, right_re, right_im):
    out_re = jnp.dot(left_re, right_re, precision=exact_mode) - jnp.dot(
        left_im, right_im, precision=exact_mode
    )
    out_im = jnp.dot(left_re, right_im, precision=exact_mode) + jnp.dot(
        left_im, right_re, precision=exact_mode
    )
    return (out_re, out_im)


def rotate(real_part, imag_part, phase_angle):
    cosine = jnp.cos(phase_angle)
    sine = jnp.sin(phase_angle)
    return (real_part * cosine - imag_part * sine, real_part * sine + imag_part * cosine)


def local_transform(real_part, imag_part, direction):
    block_rows, columns = real_part.shape
    outer_size = max(
        (divisor for divisor in range(1, math.isqrt(block_rows) + 1) if block_rows % divisor == 0)
    )
    inner_size = block_rows // outer_size
    outer_index = jnp.arange(outer_size, dtype=jnp.int32)
    inner_index = jnp.arange(inner_size, dtype=jnp.int32)
    outer_angle = (
        direction
        * 2.0
        * math.pi
        * (outer_index[:, None] * outer_index[None, :] % outer_size).astype(jnp.float32)
        / outer_size
    )
    twist_angle = (
        direction
        * 2.0
        * math.pi
        * (outer_index[:, None] * inner_index[None, :] % block_rows).astype(jnp.float32)
        / block_rows
    )
    inner_angle = (
        direction
        * 2.0
        * math.pi
        * (inner_index[:, None] * inner_index[None, :] % inner_size).astype(jnp.float32)
        / inner_size
    )
    step_re, step_im = complex_dot(
        jnp.cos(outer_angle),
        jnp.sin(outer_angle),
        real_part.reshape(outer_size, inner_size * columns),
        imag_part.reshape(outer_size, inner_size * columns),
    )
    step_re = step_re.reshape(outer_size, inner_size, columns)
    step_im = step_im.reshape(outer_size, inner_size, columns)
    step_re, step_im = rotate(step_re, step_im, twist_angle[:, :, None])
    inner_cos = jnp.cos(inner_angle)
    inner_sin = jnp.sin(inner_angle)
    out_re = jnp.einsum("sak,at->tsk", step_re, inner_cos, precision=exact_mode) - jnp.einsum(
        "sak,at->tsk", step_im, inner_sin, precision=exact_mode
    )
    out_im = jnp.einsum("sak,at->tsk", step_re, inner_sin, precision=exact_mode) + jnp.einsum(
        "sak,at->tsk", step_im, inner_cos, precision=exact_mode
    )
    return (out_re.reshape(block_rows, columns), out_im.reshape(block_rows, columns))


def convolve_channels(signal, filter_taps):
    signal_cols, taps_cols = (
        lax.all_to_all(signal, "seq", split_axis=1, concat_axis=0, tiled=True),
        lax.all_to_all(filter_taps, "seq", split_axis=1, concat_axis=0, tiled=True),
    )
    total_rows, width = signal_cols.shape
    joined = jnp.concatenate((signal_cols, taps_cols), axis=1)
    padded = jnp.concatenate((joined, jnp.zeros_like(joined)), axis=0)
    spec_re, spec_im = local_transform(padded, jnp.zeros_like(padded), -1.0)
    left_re, left_im = (spec_re[:, :width], spec_im[:, :width])
    right_re, right_im = (spec_re[:, width:], spec_im[:, width:])
    product_re = left_re * right_re - left_im * right_im
    product_im = left_re * right_im + left_im * right_re
    back_re, back_im = local_transform(product_re, product_im, 1.0)
    conv_cols = back_re[:total_rows] / (2.0 * total_rows)
    return lax.all_to_all(conv_cols, "seq", split_axis=0, concat_axis=1, tiled=True)


def pool_segments(mixed, lengths, row_of_segment, seq_index, seq_count):
    block_rows = mixed.shape[0]
    owned_rows = lengths.shape[0] // seq_count
    span_ends = jnp.cumsum(lengths)
    span_starts = span_ends - lengths
    tokens = seq_index * block_rows + jnp.arange(block_rows, dtype=jnp.int32)
    inside = (span_starts[None, :] <= tokens[:, None]) & (tokens[:, None] < span_ends[None, :])
    token_row = jnp.sum(jnp.where(inside, row_of_segment[None, :], 0), axis=1)
    wanted = jnp.arange(owned_rows * lax.axis_size("seq"), dtype=jnp.int32)
    member = (token_row[None, :] == wanted[:, None]).astype(jnp.float32)
    sums = lax.psum_scatter(
        jnp.dot(member, mixed, precision=exact_mode), "seq", scatter_dimension=0, tiled=True
    )
    mine = seq_index * owned_rows + jnp.arange(owned_rows, dtype=jnp.int32)
    seg_sizes = jnp.sum(
        jnp.where(row_of_segment[None, :] == mine[:, None], lengths[None, :], 0), axis=1
    )
    return sums / seg_sizes.astype(jnp.float32)[:, None]


def split_constant(table):
    high = table.astype(np.float32).astype(ml_dtypes.bfloat16)
    low = (table - high.astype(np.float64)).astype(np.float32).astype(ml_dtypes.bfloat16)
    return np.stack([high, low])


def transform_tables(block):
    freqs = np.concatenate([np.arange(0, block, 2), np.arange(1, block, 2)])
    turns = ((2 * freqs[:, None] + 1) * np.arange(block)[None, :]) % (4 * block)
    angle = turns * (np.pi / (2 * block))
    forward = np.concatenate([np.cos(angle), -np.sin(angle)], axis=0)
    inverse = forward.T / block
    return split_constant(forward), split_constant(inverse)


def split_value(value):
    high = value.astype(jnp.bfloat16)
    low = (value - high.astype(jnp.float32)).astype(jnp.bfloat16)
    return high, low


def mul(left, right):
    return jnp.dot(left, right, preferred_element_type=jnp.float32)


def peer_of(me, offset, count):
    peer, place = 0, 1
    while place < count:
        peer = peer + ((me // place + offset // place) % 2) * place
        place *= 2
    return peer


def mixer_kernel(
    count, block,
    lengths, rows, signal, taps, gate, skip, forward, inverse,
    mixed, pooled,
    sig_in, tap_in, sig_own, gate_own, spec_s, spec_h, prod, conv_out, conv_in, mixed_v, member, part, part_in,
    fwd_v, inv_v,
    local_sem, table_sem, gate_sem, tap_sem, send_s, recv_s, send_h, recv_h, send_c, recv_c, send_p, recv_p, out_sem,
):
    me = lax.axis_index("seq")
    tokens, width = signal.shape
    lanes = width // count
    halves = tokens // block
    blocks = halves * count
    owned = part.shape[1]
    segs = owned * count
    peers = [peer_of(me, d, count) for d in range(count)]

    def cols(index):
        return pl.ds(pl.multiple_of(index * lanes, LANES), lanes)

    fwd_copy = pltpu.make_async_copy(forward, fwd_v, table_sem.at[0])
    inv_copy = pltpu.make_async_copy(inverse, inv_v, table_sem.at[1])
    tap_copy = pltpu.make_async_copy(taps.at[:, cols(me)], tap_in.at[0], tap_sem)
    sig_copies = [
        pltpu.make_async_copy(signal.at[:, cols(peers[d])], sig_own.at[d], local_sem.at[d]) for d in range(count)
    ]
    gate_copies = [
        pltpu.make_async_copy(gate.at[:, cols(peers[d])], gate_own.at[d], gate_sem.at[d]) for d in range(count)
    ]

    barrier = pltpu.get_barrier_semaphore()
    for d in range(1, count):
        pl.semaphore_signal(barrier, inc=1, device_id={"seq": peers[d]}, device_id_type=MESH)
    fwd_copy.start()
    sig_copies[0].start()
    tap_copy.start()
    pl.semaphore_wait(barrier, count - 1)

    def remote(src, dst, send, recv, d):
        return pltpu.make_async_remote_copy(
            src_ref=src, dst_ref=dst, send_sem=send.at[d], recv_sem=recv.at[d],
            device_id={"seq": peers[d]}, device_id_type=MESH,
        )

    order = list(range(count - 1, 0, -1))
    sig_sends = {d: remote(signal.at[:, cols(peers[d])], sig_in.at[d], send_s, recv_s, d) for d in order}
    tap_sends = {d: remote(taps.at[:, cols(peers[d])], tap_in.at[d], send_h, recv_h, d) for d in order}
    for d in order:
        sig_sends[d].start()
    for d in order:
        tap_sends[d].start()
    inv_copy.start()
    for d in range(1, count):
        sig_copies[d].start()
    for d in range(count):
        gate_copies[d].start()

    token = me * tokens + lax.broadcasted_iota(jnp.int32, (8, tokens), 1)
    mine = me * owned + lax.broadcasted_iota(jnp.int32, (owned, LANES), 0)
    start = jnp.int32(0)
    token_row = jnp.zeros((8, tokens), jnp.int32)
    sizes = jnp.zeros((owned, LANES), jnp.int32)
    for k in range(segs):
        stop = start + lengths[k]
        token_row = jnp.where((token >= start) & (token < stop), rows[k], token_row)
        sizes = jnp.where(mine == rows[k], lengths[k], sizes)
        start = stop
    row_at = lax.broadcasted_iota(jnp.int32, (segs, tokens), 0)
    member[...] = (row_at == token_row[0:1, :]).astype(jnp.float32).astype(jnp.bfloat16)

    fwd_copy.wait()

    def to_spectrum(source, place, spec):
        value = source[...]
        wide = jnp.concatenate([value[h * block:(h + 1) * block] for h in range(halves)], axis=1)
        high, low = split_value(wide)
        result = mul(fwd_v[0], high) + (mul(fwd_v[1], high) + mul(fwd_v[0], low))
        for h in range(halves):
            spec[place * halves + h] = result[:, h * lanes:(h + 1) * lanes]

    sig_copies[0].wait()
    to_spectrum(sig_own.at[0], me, spec_s)
    tap_copy.wait()
    to_spectrum(tap_in.at[0], me, spec_h)
    for d in order[::-1]:
        sig_sends[d].wait_recv()
        to_spectrum(sig_in.at[d], peers[d], spec_s)
    for d in order[::-1]:
        tap_sends[d].wait_recv()
        to_spectrum(tap_in.at[d], peers[d], spec_h)

    def product_tile(sign, row):
        re = pl.ds(pl.multiple_of(row, 8), 8)
        im = pl.ds(pl.multiple_of(row + block, 8), 8)
        s_re = [spec_s[i, re, :] for i in range(blocks)]
        s_im = [spec_s[i, im, :] for i in range(blocks)]
        h_re = [spec_h[i, re, :] for i in range(blocks)]
        h_im = [spec_h[i, im, :] for i in range(blocks)]
        old_re = old_im = None
        for j in range(blocks):
            new_re = new_im = None
            for i in range(j + 1):
                k = j - i
                a = s_re[i] * h_re[k] - s_im[i] * h_im[k]
                b = s_re[i] * h_im[k] + s_im[i] * h_re[k]
                new_re = a if new_re is None else new_re + a
                new_im = b if new_im is None else new_im + b
            out_re, out_im = new_re, new_im
            if j:
                out_re = new_re - old_im if sign > 0 else new_re + old_im
                out_im = new_im + old_re if sign > 0 else new_im - old_re
            at = pl.ds((j % halves) * lanes, lanes)
            prod[j // halves, re, at] = out_re
            prod[j // halves, im, at] = out_im
            old_re, old_im = new_re, new_im

    steps = block // 16
    for sign, base in ((1, 0), (-1, block // 2)):
        def body(t, carry, sign=sign, base=base):
            product_tile(sign, base + t * 8)
            return carry
        lax.fori_loop(0, steps, body, 0)

    inv_copy.wait()

    def from_spectrum(place, target):
        high, low = split_value(prod[place])
        result = mul(inv_v[0], high) + (mul(inv_v[1], high) + mul(inv_v[0], low))
        for h in range(halves):
            target[h * block:(h + 1) * block, :] = result[:, h * lanes:(h + 1) * lanes]

    conv_sends = {d: remote(conv_out.at[d], conv_in.at[d], send_c, recv_c, d) for d in order}
    for d in order:
        from_spectrum(peers[d], conv_out.at[d])
        conv_sends[d].start()
    from_spectrum(me, conv_out.at[0])

    out_copies = []

    def finish(d, conv):
        sig_copies[d].wait() if d else None
        gate_copies[d].wait()
        gain = skip[0:1, cols(peers[d])]
        value = gate_own[d] * (conv[...] + gain * sig_own[d])
        mixed_v[d] = value
        copy = pltpu.make_async_copy(mixed_v.at[d], mixed.at[:, cols(peers[d])], out_sem.at[d])
        copy.start()
        out_copies.append(copy)
        high, low = split_value(value)
        sums = mul(member[...], high) + mul(member[...], low)
        for p in range(count):
            part[p, :, cols(peers[d])] = sums[p * owned:(p + 1) * owned]

    finish(0, conv_out.at[0])
    for d in order[::-1]:
        conv_sends[d].wait_recv()
        finish(d, conv_in.at[d])

    part_sends = {d: remote(part.at[peers[d]], part_in.at[d], send_p, recv_p, d) for d in order}
    for d in order:
        part_sends[d].start()
    total = part[me]
    for d in order:
        part_sends[d].wait_recv()
        total = total + part_in[d]
    pooled[...] = total / jnp.concatenate([sizes] * (width // LANES), axis=1).astype(jnp.float32)

    for copy in out_copies:
        copy.wait()
    for group in (sig_sends, tap_sends, conv_sends, part_sends):
        for d in order:
            group[d].wait_send()


def fits_kernel(tokens, width, count):
    return (
        count > 1
        and count & (count - 1) == 0
        and width % (count * LANES) == 0
        and tokens % (2 * LANES) == 0
    )


def fused_on_device(count, signal, filter_taps, out_gate, skip_gain, lengths, row_of_segment):
    tokens, width = signal.shape
    lanes = width // count
    block = 2 * LANES
    halves = tokens // block
    owned = lengths.shape[0] // count
    segs = owned * count
    forward, inverse = transform_tables(block)
    f32, bf16 = jnp.float32, jnp.bfloat16
    dma = pltpu.SemaphoreType.DMA
    anywhere = pl.BlockSpec(memory_space=pl.ANY)
    scalars = pl.BlockSpec(memory_space=pltpu.SMEM)
    vmem = pl.BlockSpec(memory_space=pltpu.VMEM)
    piece = pltpu.VMEM((count, tokens, lanes), f32)
    spectra = pltpu.VMEM((count * halves, 2 * block, lanes), f32)
    return pl.pallas_call(
        functools.partial(mixer_kernel, count, block),
        out_shape=(
            jax.ShapeDtypeStruct((tokens, width), f32),
            jax.ShapeDtypeStruct((owned, width), f32),
        ),
        in_specs=[scalars, scalars, anywhere, anywhere, anywhere, vmem, anywhere, anywhere],
        out_specs=(anywhere, vmem),
        scratch_shapes=[
            piece, piece, piece, piece, spectra, spectra,
            pltpu.VMEM((count, 2 * block, halves * lanes), f32),
            piece, piece, piece,
            pltpu.VMEM((segs, tokens), bf16),
            pltpu.VMEM((count, owned, width), f32),
            pltpu.VMEM((count, owned, width), f32),
            pltpu.VMEM(forward.shape, bf16),
            pltpu.VMEM(inverse.shape, bf16),
            dma((count,)), dma((2,)), dma((count,)), dma,
            dma((count,)), dma((count,)), dma((count,)), dma((count,)),
            dma((count,)), dma((count,)), dma((count,)), dma((count,)),
            dma((count,)),
        ],
        compiler_params=pltpu.CompilerParams(
            collective_id=0, has_side_effects=True, vmem_limit_bytes=40 * 1024 * 1024
        ),
        name="mixer",
    )(
        lengths, row_of_segment, signal, filter_taps, out_gate, skip_gain[None, :],
        jnp.asarray(forward), jnp.asarray(inverse),
    )


def on_device(signal, filter_taps, out_gate, skip_gain, lengths, row_of_segment):
    seq_count = lax.axis_size("seq")
    if fits_kernel(signal.shape[0], signal.shape[1], seq_count):
        return fused_on_device(
            seq_count, signal, filter_taps, out_gate, skip_gain, lengths, row_of_segment
        )
    seq_index = lax.axis_index("seq")
    conv = convolve_channels(signal, filter_taps)
    mixed = out_gate * (conv + skip_gain[None, :] * signal)
    pooled = pool_segments(mixed, lengths, row_of_segment, seq_index, seq_count)
    return (mixed, pooled)


def solution(mesh):
    placed = (P("seq", "chan"), P("seq", "chan"), P("seq", "chan"), P("chan"), P(), P())
    return jax.shard_map(
        on_device,
        mesh=mesh,
        in_specs=placed,
        out_specs=(P("seq", "chan"), P("seq", "chan")),
        check_vma=False,
    )
```

```python
import functools
import math

import jax
import jax.numpy as jnp
import ml_dtypes
import numpy as np
from jax import lax
from jax.experimental import pallas as pl
from jax.experimental.pallas import tpu as pltpu
from jax.sharding import PartitionSpec as P

LANES = 128
MESH = pl.DeviceIdType.MESH

exact_mode = lax.Precision.HIGHEST


def complex_dot(left_re, left_im, right_re, right_im):
    out_re = jnp.dot(left_re, right_re, precision=exact_mode) - jnp.dot(
        left_im, right_im, precision=exact_mode
    )
    out_im = jnp.dot(left_re, right_im, precision=exact_mode) + jnp.dot(
        left_im, right_re, precision=exact_mode
    )
    return (out_re, out_im)


def rotate(real_part, imag_part, phase_angle):
    cosine = jnp.cos(phase_angle)
    sine = jnp.sin(phase_angle)
    return (real_part * cosine - imag_part * sine, real_part * sine + imag_part * cosine)


def local_transform(real_part, imag_part, direction):
    block_rows, columns = real_part.shape
    outer_size = max(
        (divisor for divisor in range(1, math.isqrt(block_rows) + 1) if block_rows % divisor == 0)
    )
    inner_size = block_rows // outer_size
    outer_index = jnp.arange(outer_size, dtype=jnp.int32)
    inner_index = jnp.arange(inner_size, dtype=jnp.int32)
    outer_angle = (
        direction
        * 2.0
        * math.pi
        * (outer_index[:, None] * outer_index[None, :] % outer_size).astype(jnp.float32)
        / outer_size
    )
    twist_angle = (
        direction
        * 2.0
        * math.pi
        * (outer_index[:, None] * inner_index[None, :] % block_rows).astype(jnp.float32)
        / block_rows
    )
    inner_angle = (
        direction
        * 2.0
        * math.pi
        * (inner_index[:, None] * inner_index[None, :] % inner_size).astype(jnp.float32)
        / inner_size
    )
    step_re, step_im = complex_dot(
        jnp.cos(outer_angle),
        jnp.sin(outer_angle),
        real_part.reshape(outer_size, inner_size * columns),
        imag_part.reshape(outer_size, inner_size * columns),
    )
    step_re = step_re.reshape(outer_size, inner_size, columns)
    step_im = step_im.reshape(outer_size, inner_size, columns)
    step_re, step_im = rotate(step_re, step_im, twist_angle[:, :, None])
    inner_cos = jnp.cos(inner_angle)
    inner_sin = jnp.sin(inner_angle)
    out_re = jnp.einsum("sak,at->tsk", step_re, inner_cos, precision=exact_mode) - jnp.einsum(
        "sak,at->tsk", step_im, inner_sin, precision=exact_mode
    )
    out_im = jnp.einsum("sak,at->tsk", step_re, inner_sin, precision=exact_mode) + jnp.einsum(
        "sak,at->tsk", step_im, inner_cos, precision=exact_mode
    )
    return (out_re.reshape(block_rows, columns), out_im.reshape(block_rows, columns))


def convolve_channels(signal, filter_taps):
    signal_cols, taps_cols = (
        lax.all_to_all(signal, "seq", split_axis=1, concat_axis=0, tiled=True),
        lax.all_to_all(filter_taps, "seq", split_axis=1, concat_axis=0, tiled=True),
    )
    total_rows, width = signal_cols.shape
    joined = jnp.concatenate((signal_cols, taps_cols), axis=1)
    padded = jnp.concatenate((joined, jnp.zeros_like(joined)), axis=0)
    spec_re, spec_im = local_transform(padded, jnp.zeros_like(padded), -1.0)
    left_re, left_im = (spec_re[:, :width], spec_im[:, :width])
    right_re, right_im = (spec_re[:, width:], spec_im[:, width:])
    product_re = left_re * right_re - left_im * right_im
    product_im = left_re * right_im + left_im * right_re
    back_re, back_im = local_transform(product_re, product_im, 1.0)
    conv_cols = back_re[:total_rows] / (2.0 * total_rows)
    return lax.all_to_all(conv_cols, "seq", split_axis=0, concat_axis=1, tiled=True)


def pool_segments(mixed, lengths, row_of_segment, seq_index, seq_count):
    block_rows = mixed.shape[0]
    owned_rows = lengths.shape[0] // seq_count
    span_ends = jnp.cumsum(lengths)
    span_starts = span_ends - lengths
    tokens = seq_index * block_rows + jnp.arange(block_rows, dtype=jnp.int32)
    inside = (span_starts[None, :] <= tokens[:, None]) & (tokens[:, None] < span_ends[None, :])
    token_row = jnp.sum(jnp.where(inside, row_of_segment[None, :], 0), axis=1)
    wanted = jnp.arange(owned_rows * lax.axis_size("seq"), dtype=jnp.int32)
    member = (token_row[None, :] == wanted[:, None]).astype(jnp.float32)
    sums = lax.psum_scatter(
        jnp.dot(member, mixed, precision=exact_mode), "seq", scatter_dimension=0, tiled=True
    )
    mine = seq_index * owned_rows + jnp.arange(owned_rows, dtype=jnp.int32)
    seg_sizes = jnp.sum(
        jnp.where(row_of_segment[None, :] == mine[:, None], lengths[None, :], 0), axis=1
    )
    return sums / seg_sizes.astype(jnp.float32)[:, None]


def split_constant(table):
    high = table.astype(np.float32).astype(ml_dtypes.bfloat16)
    low = (table - high.astype(np.float64)).astype(np.float32).astype(ml_dtypes.bfloat16)
    return np.stack([high, low])


def transform_tables(block):
    freqs = np.concatenate([np.arange(0, block, 2), np.arange(1, block, 2)])
    turns = ((2 * freqs[:, None] + 1) * np.arange(block)[None, :]) % (4 * block)
    angle = turns * (np.pi / (2 * block))
    forward = np.concatenate([np.cos(angle), -np.sin(angle)], axis=0)
    inverse = forward.T / block
    return split_constant(forward), split_constant(inverse)


def split_value(value):
    high = value.astype(jnp.bfloat16)
    low = (value - high.astype(jnp.float32)).astype(jnp.bfloat16)
    return high, low


def mul(left, right):
    return jnp.dot(left, right, preferred_element_type=jnp.float32)


def peer_of(me, offset, count):
    peer, place = 0, 1
    while place < count:
        peer = peer + ((me // place + offset // place) % 2) * place
        place *= 2
    return peer


def mixer_kernel(
    count, block,
    lengths_at, rows_at, signal, taps, gate, skip_at, forward, inverse,
    mixed, pooled,
    sig_in, tap_in, sig_own, gate_own, spec_s, spec_h, prod, carry, conv_out, conv_in, mixed_v, member, part, part_in,
    fwd_v, inv_v, lengths, rows, skip,
    local_sem, table_sem, gate_sem, tap_sem, send_s, recv_s, send_h, recv_h, send_c, recv_c, send_p, recv_p, out_sem,
):
    me = lax.axis_index("seq")
    tokens, width = signal.shape
    lanes = width // count
    halves = tokens // block
    blocks = halves * count
    owned = part.shape[1]
    segs = owned * count
    peers = [peer_of(me, d, count) for d in range(count)]
    pieces = [pl.ds(h * block, block) for h in range(halves)]

    def cols(index):
        return pl.ds(pl.multiple_of(index * lanes, LANES), lanes)

    table_copies = [
        pltpu.make_async_copy(source, target, table_sem.at[i])
        for i, (source, target) in enumerate(
            ((forward, fwd_v), (inverse, inv_v), (lengths_at, lengths), (rows_at, rows), (skip_at, skip))
        )
    ]
    fwd_copy, inv_copy, len_copy, row_copy, skip_copy = table_copies
    tap_copy = pltpu.make_async_copy(taps.at[:, cols(me)], tap_in.at[0], tap_sem)
    sig_copies = [
        pltpu.make_async_copy(signal.at[:, cols(peers[d])], sig_own.at[d], local_sem.at[d]) for d in range(count)
    ]
    gate_copies = [
        pltpu.make_async_copy(gate.at[:, cols(peers[d])], gate_own.at[d], gate_sem.at[d]) for d in range(count)
    ]

    barrier = pltpu.get_barrier_semaphore()
    for d in range(1, count):
        pl.semaphore_signal(barrier, inc=1, device_id={"seq": peers[d]}, device_id_type=MESH)
    fwd_copy.start()
    sig_copies[0].start()
    tap_copy.start()
    len_copy.start()
    row_copy.start()
    pl.semaphore_wait(barrier, count - 1)

    def remote(src, dst, send, recv, peer):
        return pltpu.make_async_remote_copy(
            src_ref=src, dst_ref=dst, send_sem=send, recv_sem=recv,
            device_id={"seq": peer}, device_id_type=MESH,
        )

    def scatter(source, target, send, recv):
        return {
            (d, h): remote(
                source.at[pieces[h], cols(peers[d])], target.at[d, pieces[h], :],
                send.at[d, h], recv.at[d, h], peers[d],
            )
            for h in range(halves)
            for d in order
        }

    order = list(range(count - 1, 0, -1))
    sig_sends = scatter(signal, sig_in, send_s, recv_s)
    tap_sends = scatter(taps, tap_in, send_h, recv_h)
    for copy in sig_sends.values():
        copy.start()
    for copy in tap_sends.values():
        copy.start()
    inv_copy.start()
    skip_copy.start()
    for d in range(1, count):
        sig_copies[d].start()
    for d in range(count):
        gate_copies[d].start()

    len_copy.wait()
    row_copy.wait()
    token = me * tokens + lax.broadcasted_iota(jnp.int32, (8, tokens), 1)
    mine = me * owned + lax.broadcasted_iota(jnp.int32, (owned, LANES), 0)
    start = jnp.int32(0)
    token_row = jnp.zeros((8, tokens), jnp.int32)
    sizes = jnp.zeros((owned, LANES), jnp.int32)
    for k in range(segs):
        stop = start + lengths[k]
        token_row = jnp.where((token >= start) & (token < stop), rows[k], token_row)
        sizes = jnp.where(mine == rows[k], lengths[k], sizes)
        start = stop
    row_at = lax.broadcasted_iota(jnp.int32, (segs, tokens), 0)
    member[...] = (row_at == token_row[0:1, :]).astype(jnp.float32).astype(jnp.bfloat16)

    fwd_copy.wait()

    def to_spectrum(source, place, spec):
        value = source[...]
        wide = jnp.concatenate([value[h * block:(h + 1) * block] for h in range(halves)], axis=1)
        high, low = split_value(wide)
        result = mul(fwd_v[0], high) + (mul(fwd_v[1], high) + mul(fwd_v[0], low))
        for h in range(halves):
            spec[place * halves + h] = result[:, h * lanes:(h + 1) * lanes]

    sig_copies[0].wait()
    to_spectrum(sig_own.at[0], me, spec_s)
    tap_copy.wait()
    to_spectrum(tap_in.at[0], me, spec_h)
    for sends, source, spec in ((sig_sends, sig_in, spec_s), (tap_sends, tap_in, spec_h)):
        for d in order[::-1]:
            for h in range(halves):
                sends[d, h].wait_recv()
            to_spectrum(source.at[d], peers[d], spec)

    def product_tile(sign, row, first, last):
        re = pl.ds(pl.multiple_of(row, 8), 8)
        im = pl.ds(pl.multiple_of(row + block, 8), 8)
        s_re = [spec_s[i, re, :] for i in range(last)]
        s_im = [spec_s[i, im, :] for i in range(last)]
        h_re = [spec_h[i, re, :] for i in range(last)]
        h_im = [spec_h[i, im, :] for i in range(last)]
        old_re, old_im = (carry[re, :], carry[im, :]) if first else (None, None)
        for j in range(first, last):
            new_re = new_im = None
            for i in range(j + 1):
                k = j - i
                a = s_re[i] * h_re[k] - s_im[i] * h_im[k]
                b = s_re[i] * h_im[k] + s_im[i] * h_re[k]
                new_re = a if new_re is None else new_re + a
                new_im = b if new_im is None else new_im + b
            out_re, out_im = new_re, new_im
            if j:
                out_re = new_re - old_im if sign > 0 else new_re + old_im
                out_im = new_im + old_re if sign > 0 else new_im - old_re
            at = pl.ds((j % halves) * lanes, lanes)
            prod[j // halves, re, at] = out_re
            prod[j // halves, im, at] = out_im
            old_re, old_im = new_re, new_im
        if last < blocks:
            carry[re, :] = old_re
            carry[im, :] = old_im

    def products(first, last):
        for sign, base in ((1, 0), (-1, block // 2)):
            def body(t, state, sign=sign, base=base):
                product_tile(sign, base + t * 8, first, last)
                return state
            lax.fori_loop(0, block // 16, body, 0)

    def back_copy(d, h, peer):
        return remote(
            conv_out.at[d, pieces[h], :], conv_in.at[d, pieces[h], :], send_c.at[d, h], recv_c.at[d, h], peer
        )

    def give_back(owner):
        high, low = split_value(prod[owner])
        result = mul(inv_v[0], high) + (mul(inv_v[1], high) + mul(inv_v[0], low))
        d = peer_of(me, owner, count)
        for h in range(halves):
            conv_out[d, pieces[h], :] = result[:, h * lanes:(h + 1) * lanes]

        @pl.when(me != owner)
        def _():
            for h in range(halves):
                back_copy(d, h, owner).start()

    inv_copy.wait()
    products(0, blocks // 2)
    for owner in range(count // 2):
        give_back(owner)
    products(blocks // 2, blocks)
    for owner in range(count // 2, count):
        give_back(owner)

    out_copies = []

    def finish(d, h, conv):
        at = cols(peers[d])
        value = gate_own[d, pieces[h], :] * (conv[d, pieces[h], :] + skip[:, at] * sig_own[d, pieces[h], :])
        mixed_v[d, pieces[h], :] = value
        copy = pltpu.make_async_copy(mixed_v.at[d, pieces[h], :], mixed.at[pieces[h], at], out_sem.at[d, h])
        copy.start()
        out_copies.append(copy)
        high, low = split_value(value)
        inside = member[:, h * block:(h + 1) * block]
        sums = mul(inside, high) + mul(inside, low)
        for p in range(count):
            new = sums[p * owned:(p + 1) * owned]
            part[p, :, at] = part[p, :, at] + new if h else new

    skip_copy.wait()
    for d in range(count):
        if d:
            sig_copies[d].wait()
        gate_copies[d].wait()
        for h in range(halves):
            if d:
                back_copy(d, h, peers[d]).wait_recv()
            finish(d, h, conv_in if d else conv_out)

    part_sends = [
        remote(part.at[peers[d]], part_in.at[d], send_p.at[d], recv_p.at[d], peers[d]) for d in order
    ]
    for copy in part_sends:
        copy.start()
    total = part[me]
    for d, copy in zip(order, part_sends):
        copy.wait_recv()
        total = total + part_in[d]
    pooled[...] = total / jnp.concatenate([sizes] * (width // LANES), axis=1).astype(jnp.float32)

    for copy in out_copies:
        copy.wait()
    for copy in [*sig_sends.values(), *tap_sends.values(), *part_sends]:
        copy.wait_send()
    for d in order:
        for h in range(halves):
            back_copy(d, h, peers[d]).wait_send()


def fits_kernel(tokens, width, count):
    return (
        count > 1
        and count & (count - 1) == 0
        and width % (count * LANES) == 0
        and tokens % (2 * LANES) == 0
    )


def fused_on_device(count, signal, filter_taps, out_gate, skip_gain, lengths, row_of_segment):
    tokens, width = signal.shape
    lanes = width // count
    block = 2 * LANES
    halves = tokens // block
    owned = lengths.shape[0] // count
    segs = owned * count
    forward, inverse = transform_tables(block)
    f32, bf16 = jnp.float32, jnp.bfloat16
    dma = pltpu.SemaphoreType.DMA
    each = dma((count, halves))
    anywhere = pl.BlockSpec(memory_space=pl.ANY)
    vmem = pl.BlockSpec(memory_space=pltpu.VMEM)
    piece = pltpu.VMEM((count, tokens, lanes), f32)
    spectra = pltpu.VMEM((count * halves, 2 * block, lanes), f32)
    return pl.pallas_call(
        functools.partial(mixer_kernel, count, block),
        out_shape=(
            jax.ShapeDtypeStruct((tokens, width), f32),
            jax.ShapeDtypeStruct((owned, width), f32),
        ),
        in_specs=[anywhere] * 8,
        out_specs=(anywhere, vmem),
        scratch_shapes=[
            piece, piece, piece, piece, spectra, spectra,
            pltpu.VMEM((count, 2 * block, halves * lanes), f32),
            pltpu.VMEM((2 * block, lanes), f32),
            piece, piece, piece,
            pltpu.VMEM((segs, tokens), bf16),
            pltpu.VMEM((count, owned, width), f32),
            pltpu.VMEM((count, owned, width), f32),
            pltpu.VMEM(forward.shape, bf16),
            pltpu.VMEM(inverse.shape, bf16),
            pltpu.SMEM(lengths.shape, jnp.int32),
            pltpu.SMEM(lengths.shape, jnp.int32),
            pltpu.VMEM((1, width), f32),
            dma((count,)), dma((5,)), dma((count,)), dma,
            each, each, each, each, each, each,
            dma((count,)), dma((count,)), each,
        ],
        compiler_params=pltpu.CompilerParams(
            collective_id=0, has_side_effects=True, vmem_limit_bytes=64 * 1024 * 1024
        ),
        name="mixer",
    )(
        lengths, row_of_segment, signal, filter_taps, out_gate, skip_gain[None, :],
        jnp.asarray(forward), jnp.asarray(inverse),
    )


def on_device(signal, filter_taps, out_gate, skip_gain, lengths, row_of_segment):
    seq_count = lax.axis_size("seq")
    if fits_kernel(signal.shape[0], signal.shape[1], seq_count):
        return fused_on_device(
            seq_count, signal, filter_taps, out_gate, skip_gain, lengths, row_of_segment
        )
    seq_index = lax.axis_index("seq")
    conv = convolve_channels(signal, filter_taps)
    mixed = out_gate * (conv + skip_gain[None, :] * signal)
    pooled = pool_segments(mixed, lengths, row_of_segment, seq_index, seq_count)
    return (mixed, pooled)


def solution(mesh):
    placed = (P("seq", "chan"), P("seq", "chan"), P("seq", "chan"), P("chan"), P(), P())
    return jax.shard_map(
        on_device,
        mesh=mesh,
        in_specs=placed,
        out_specs=(P("seq", "chan"), P("seq", "chan")),
        check_vma=False,
    )
```

```python
import functools
import math

import jax
import jax.numpy as jnp
import ml_dtypes
import numpy as np
from jax import lax
from jax.experimental import pallas as pl
from jax.experimental.pallas import tpu as pltpu
from jax.sharding import PartitionSpec as P

LANES = 128
MESH = pl.DeviceIdType.MESH

exact_mode = lax.Precision.HIGHEST


def complex_dot(left_re, left_im, right_re, right_im):
    out_re = jnp.dot(left_re, right_re, precision=exact_mode) - jnp.dot(
        left_im, right_im, precision=exact_mode
    )
    out_im = jnp.dot(left_re, right_im, precision=exact_mode) + jnp.dot(
        left_im, right_re, precision=exact_mode
    )
    return (out_re, out_im)


def rotate(real_part, imag_part, phase_angle):
    cosine = jnp.cos(phase_angle)
    sine = jnp.sin(phase_angle)
    return (real_part * cosine - imag_part * sine, real_part * sine + imag_part * cosine)


def local_transform(real_part, imag_part, direction):
    block_rows, columns = real_part.shape
    outer_size = max(
        (divisor for divisor in range(1, math.isqrt(block_rows) + 1) if block_rows % divisor == 0)
    )
    inner_size = block_rows // outer_size
    outer_index = jnp.arange(outer_size, dtype=jnp.int32)
    inner_index = jnp.arange(inner_size, dtype=jnp.int32)
    outer_angle = (
        direction
        * 2.0
        * math.pi
        * (outer_index[:, None] * outer_index[None, :] % outer_size).astype(jnp.float32)
        / outer_size
    )
    twist_angle = (
        direction
        * 2.0
        * math.pi
        * (outer_index[:, None] * inner_index[None, :] % block_rows).astype(jnp.float32)
        / block_rows
    )
    inner_angle = (
        direction
        * 2.0
        * math.pi
        * (inner_index[:, None] * inner_index[None, :] % inner_size).astype(jnp.float32)
        / inner_size
    )
    step_re, step_im = complex_dot(
        jnp.cos(outer_angle),
        jnp.sin(outer_angle),
        real_part.reshape(outer_size, inner_size * columns),
        imag_part.reshape(outer_size, inner_size * columns),
    )
    step_re = step_re.reshape(outer_size, inner_size, columns)
    step_im = step_im.reshape(outer_size, inner_size, columns)
    step_re, step_im = rotate(step_re, step_im, twist_angle[:, :, None])
    inner_cos = jnp.cos(inner_angle)
    inner_sin = jnp.sin(inner_angle)
    out_re = jnp.einsum("sak,at->tsk", step_re, inner_cos, precision=exact_mode) - jnp.einsum(
        "sak,at->tsk", step_im, inner_sin, precision=exact_mode
    )
    out_im = jnp.einsum("sak,at->tsk", step_re, inner_sin, precision=exact_mode) + jnp.einsum(
        "sak,at->tsk", step_im, inner_cos, precision=exact_mode
    )
    return (out_re.reshape(block_rows, columns), out_im.reshape(block_rows, columns))


def convolve_channels(signal, filter_taps):
    signal_cols, taps_cols = (
        lax.all_to_all(signal, "seq", split_axis=1, concat_axis=0, tiled=True),
        lax.all_to_all(filter_taps, "seq", split_axis=1, concat_axis=0, tiled=True),
    )
    total_rows, width = signal_cols.shape
    joined = jnp.concatenate((signal_cols, taps_cols), axis=1)
    padded = jnp.concatenate((joined, jnp.zeros_like(joined)), axis=0)
    spec_re, spec_im = local_transform(padded, jnp.zeros_like(padded), -1.0)
    left_re, left_im = (spec_re[:, :width], spec_im[:, :width])
    right_re, right_im = (spec_re[:, width:], spec_im[:, width:])
    product_re = left_re * right_re - left_im * right_im
    product_im = left_re * right_im + left_im * right_re
    back_re, back_im = local_transform(product_re, product_im, 1.0)
    conv_cols = back_re[:total_rows] / (2.0 * total_rows)
    return lax.all_to_all(conv_cols, "seq", split_axis=0, concat_axis=1, tiled=True)


def pool_segments(mixed, lengths, row_of_segment, seq_index, seq_count):
    block_rows = mixed.shape[0]
    owned_rows = lengths.shape[0] // seq_count
    span_ends = jnp.cumsum(lengths)
    span_starts = span_ends - lengths
    tokens = seq_index * block_rows + jnp.arange(block_rows, dtype=jnp.int32)
    inside = (span_starts[None, :] <= tokens[:, None]) & (tokens[:, None] < span_ends[None, :])
    token_row = jnp.sum(jnp.where(inside, row_of_segment[None, :], 0), axis=1)
    wanted = jnp.arange(owned_rows * lax.axis_size("seq"), dtype=jnp.int32)
    member = (token_row[None, :] == wanted[:, None]).astype(jnp.float32)
    sums = lax.psum_scatter(
        jnp.dot(member, mixed, precision=exact_mode), "seq", scatter_dimension=0, tiled=True
    )
    mine = seq_index * owned_rows + jnp.arange(owned_rows, dtype=jnp.int32)
    seg_sizes = jnp.sum(
        jnp.where(row_of_segment[None, :] == mine[:, None], lengths[None, :], 0), axis=1
    )
    return sums / seg_sizes.astype(jnp.float32)[:, None]


def split_constant(table):
    high = table.astype(np.float32).astype(ml_dtypes.bfloat16)
    low = (table - high.astype(np.float64)).astype(np.float32).astype(ml_dtypes.bfloat16)
    return np.stack([high, low])


def transform_tables(block):
    freqs = np.concatenate([np.arange(0, block, 2), np.arange(1, block, 2)])
    turns = ((2 * freqs[:, None] + 1) * np.arange(block)[None, :]) % (4 * block)
    angle = turns * (np.pi / (2 * block))
    forward = np.concatenate([np.cos(angle), -np.sin(angle)], axis=0)
    inverse = forward.T / block
    return split_constant(forward), split_constant(inverse)


def split_value(value):
    high = value.astype(jnp.bfloat16)
    low = (value - high.astype(jnp.float32)).astype(jnp.bfloat16)
    return high, low


def mul(left, right):
    return jnp.dot(left, right, preferred_element_type=jnp.float32)


def peer_of(me, offset, count):
    peer, place = 0, 1
    while place < count:
        peer = peer + ((me // place + offset // place) % 2) * place
        place *= 2
    return peer


def mixer_kernel(
    count, block,
    lengths_at, rows_at, signal, taps, gate, skip_at, forward, inverse,
    mixed, pooled,
    sig_in, tap_in, sig_own, gate_own, spec_s, spec_h, prod, acc, conv_out, conv_in, mixed_v, member, part, part_in,
    fwd_v, inv_v, lengths, rows, skip,
    local_sem, table_sem, gate_sem, tap_sem, send_s, recv_s, send_h, recv_h, send_c, recv_c, send_p, recv_p, out_sem,
):
    me = lax.axis_index("seq")
    tokens, width = signal.shape
    lanes = width // count
    halves = tokens // block
    blocks = halves * count
    owned = part.shape[1]
    segs = owned * count
    peers = [peer_of(me, d, count) for d in range(count)]
    pieces = [pl.ds(h * block, block) for h in range(halves)]

    def cols(index):
        return pl.ds(pl.multiple_of(index * lanes, LANES), lanes)

    table_copies = [
        pltpu.make_async_copy(source, target, table_sem.at[i])
        for i, (source, target) in enumerate(
            ((forward, fwd_v), (inverse, inv_v), (lengths_at, lengths), (rows_at, rows), (skip_at, skip))
        )
    ]
    fwd_copy, inv_copy, len_copy, row_copy, skip_copy = table_copies
    tap_copy = pltpu.make_async_copy(taps.at[:, cols(me)], tap_in.at[0], tap_sem)
    sig_copies = [
        pltpu.make_async_copy(signal.at[:, cols(peers[d])], sig_own.at[d], local_sem.at[d]) for d in range(count)
    ]
    gate_copies = [
        pltpu.make_async_copy(gate.at[:, cols(peers[d])], gate_own.at[d], gate_sem.at[d]) for d in range(count)
    ]

    barrier = pltpu.get_barrier_semaphore()
    for d in range(1, count):
        pl.semaphore_signal(barrier, inc=1, device_id={"seq": peers[d]}, device_id_type=MESH)
    fwd_copy.start()
    sig_copies[0].start()
    tap_copy.start()
    len_copy.start()
    row_copy.start()
    pl.semaphore_wait(barrier, count - 1)

    def remote(src, dst, send, recv, peer):
        return pltpu.make_async_remote_copy(
            src_ref=src, dst_ref=dst, send_sem=send, recv_sem=recv,
            device_id={"seq": peer}, device_id_type=MESH,
        )

    def scatter(source, target, send, recv):
        return {
            (d, h): remote(
                source.at[pieces[h], cols(peers[d])], target.at[d, pieces[h], :],
                send.at[d, h], recv.at[d, h], peers[d],
            )
            for h in range(halves)
            for d in order
        }

    order = list(range(count - 1, 0, -1))
    sig_sends = scatter(signal, sig_in, send_s, recv_s)
    tap_sends = scatter(taps, tap_in, send_h, recv_h)
    for copy in sig_sends.values():
        copy.start()
    inv_copy.start()
    skip_copy.start()
    for d in range(1, count):
        sig_copies[d].start()
    for d in range(count):
        gate_copies[d].start()

    len_copy.wait()
    row_copy.wait()
    token = me * tokens + lax.broadcasted_iota(jnp.int32, (8, tokens), 1)
    mine = me * owned + lax.broadcasted_iota(jnp.int32, (owned, LANES), 0)
    start = jnp.int32(0)
    token_row = jnp.zeros((8, tokens), jnp.int32)
    sizes = jnp.zeros((owned, LANES), jnp.int32)
    for k in range(segs):
        stop = start + lengths[k]
        token_row = jnp.where((token >= start) & (token < stop), rows[k], token_row)
        sizes = jnp.where(mine == rows[k], lengths[k], sizes)
        start = stop
    row_at = lax.broadcasted_iota(jnp.int32, (segs, tokens), 0)
    member[...] = (row_at == token_row[0:1, :]).astype(jnp.float32).astype(jnp.bfloat16)

    fwd_copy.wait()

    def to_spectrum(source, index, spec):
        high, low = split_value(source[...])
        both = mul(fwd_v[0], jnp.concatenate([high, low], axis=1))
        spec[index] = both[:, :lanes] + (both[:, lanes:] + mul(fwd_v[1], high))

    sig_copies[0].wait()
    for h in range(halves):
        to_spectrum(sig_own.at[0, pieces[h], :], me * halves + h, spec_s)
    tap_copy.wait()
    for h in range(halves):
        to_spectrum(tap_in.at[0, pieces[h], :], me * halves + h, spec_h)
    for h in range(halves):
        for d in order:
            sig_sends[d, h].wait_recv()
            tap_sends[d, h].start()
        for d in order:
            to_spectrum(sig_in.at[d, pieces[h], :], peers[d] * halves + h, spec_s)

    def take_taps(h):
        for d in order:
            tap_sends[d, h].wait_recv()
            to_spectrum(tap_in.at[d, pieces[h], :], peers[d] * halves + h, spec_h)

    def load(spec, wanted, re, im):
        return {i: (spec[i, re, :], spec[i, im, :]) for i in wanted}

    def products(first, last, lags, final):
        def tile(sign, row):
            re = pl.ds(pl.multiple_of(row, 8), 8)
            im = pl.ds(pl.multiple_of(row + block, 8), 8)
            used = [k for k in lags if k < last]
            taps_at = load(spec_h, used, re, im)
            sig_at = load(spec_s, sorted({j - k for j in range(first, last) for k in used if k <= j}), re, im)
            old = (acc[first - 1, re, :], acc[first - 1, im, :]) if final and first else None
            for j in range(first, last):
                total = (acc[j, re, :], acc[j, im, :]) if final else None
                for k in used:
                    if k <= j:
                        (a, b), (c, d) = sig_at[j - k], taps_at[k]
                        new = (a * c - b * d, a * d + b * c)
                        total = new if total is None else (total[0] + new[0], total[1] + new[1])
                if not final:
                    acc[j, re, :], acc[j, im, :] = total
                    continue
                out = total
                if j:
                    out = (total[0] - sign * old[1], total[1] + sign * old[0])
                at = pl.ds((j % halves) * lanes, lanes)
                prod[j // halves, re, at], prod[j // halves, im, at] = out
                old = total
            if final and last < blocks:
                acc[last - 1, re, :], acc[last - 1, im, :] = old

        for sign, base in ((1, 0), (-1, block // 2)):
            def body(t, state, sign=sign, base=base):
                tile(sign, base + t * 8)
                return state
            lax.fori_loop(0, block // 16, body, 0)

    for h in range(halves - 1):
        take_taps(h)
    products(0, blocks, [k for k in range(blocks) if k % halves < halves - 1], False)
    take_taps(halves - 1)
    late_lags = [k for k in range(blocks) if k % halves == halves - 1]

    def back_copy(d, h, peer):
        return remote(
            conv_out.at[d, pieces[h], :], conv_in.at[d, pieces[h], :], send_c.at[d, h], recv_c.at[d, h], peer
        )

    def give_back(owner):
        high, low = split_value(prod[owner])
        result = mul(inv_v[0], high) + (mul(inv_v[1], high) + mul(inv_v[0], low))
        d = peer_of(me, owner, count)
        for h in range(halves):
            conv_out[d, pieces[h], :] = result[:, h * lanes:(h + 1) * lanes]

        @pl.when(me != owner)
        def _():
            for h in range(halves):
                back_copy(d, h, owner).start()

    inv_copy.wait()
    products(0, blocks // 2, late_lags, True)
    for owner in range(count // 2):
        give_back(owner)
    products(blocks // 2, blocks, late_lags, True)
    for owner in range(count // 2, count):
        give_back(owner)

    out_copies = []

    def finish(d, h, conv):
        at = cols(peers[d])
        value = gate_own[d, pieces[h], :] * (conv[d, pieces[h], :] + skip[:, at] * sig_own[d, pieces[h], :])
        mixed_v[d, pieces[h], :] = value
        copy = pltpu.make_async_copy(mixed_v.at[d, pieces[h], :], mixed.at[pieces[h], at], out_sem.at[d, h])
        copy.start()
        out_copies.append(copy)
        high, low = split_value(value)
        inside = member[:, h * block:(h + 1) * block]
        sums = mul(inside, high) + mul(inside, low)
        for p in range(count):
            new = sums[p * owned:(p + 1) * owned]
            part[p, :, at] = part[p, :, at] + new if h else new

    skip_copy.wait()
    for d in range(count):
        if d:
            sig_copies[d].wait()
        gate_copies[d].wait()
        for h in range(halves):
            if d:
                back_copy(d, h, peers[d]).wait_recv()
            finish(d, h, conv_in if d else conv_out)

    part_sends = [
        remote(part.at[peers[d]], part_in.at[d], send_p.at[d], recv_p.at[d], peers[d]) for d in order
    ]
    for copy in part_sends:
        copy.start()
    total = part[me]
    for d, copy in zip(order, part_sends):
        copy.wait_recv()
        total = total + part_in[d]
    pooled[...] = total / jnp.concatenate([sizes] * (width // LANES), axis=1).astype(jnp.float32)

    for copy in out_copies:
        copy.wait()
    for copy in [*sig_sends.values(), *tap_sends.values(), *part_sends]:
        copy.wait_send()
    for d in order:
        for h in range(halves):
            back_copy(d, h, peers[d]).wait_send()


def fits_kernel(tokens, width, count):
    return (
        count > 1
        and count & (count - 1) == 0
        and width % (count * LANES) == 0
        and tokens % (4 * LANES) == 0
    )


def fused_on_device(count, signal, filter_taps, out_gate, skip_gain, lengths, row_of_segment):
    tokens, width = signal.shape
    lanes = width // count
    block = 2 * LANES
    halves = tokens // block
    owned = lengths.shape[0] // count
    segs = owned * count
    forward, inverse = transform_tables(block)
    f32, bf16 = jnp.float32, jnp.bfloat16
    dma = pltpu.SemaphoreType.DMA
    each = dma((count, halves))
    anywhere = pl.BlockSpec(memory_space=pl.ANY)
    vmem = pl.BlockSpec(memory_space=pltpu.VMEM)
    piece = pltpu.VMEM((count, tokens, lanes), f32)
    spectra = pltpu.VMEM((count * halves, 2 * block, lanes), f32)
    return pl.pallas_call(
        functools.partial(mixer_kernel, count, block),
        out_shape=(
            jax.ShapeDtypeStruct((tokens, width), f32),
            jax.ShapeDtypeStruct((owned, width), f32),
        ),
        in_specs=[anywhere] * 8,
        out_specs=(anywhere, vmem),
        scratch_shapes=[
            piece, piece, piece, piece, spectra, spectra,
            pltpu.VMEM((count, 2 * block, halves * lanes), f32),
            spectra,
            piece, piece, piece,
            pltpu.VMEM((segs, tokens), bf16),
            pltpu.VMEM((count, owned, width), f32),
            pltpu.VMEM((count, owned, width), f32),
            pltpu.VMEM(forward.shape, bf16),
            pltpu.VMEM(inverse.shape, bf16),
            pltpu.SMEM(lengths.shape, jnp.int32),
            pltpu.SMEM(lengths.shape, jnp.int32),
            pltpu.VMEM((1, width), f32),
            dma((count,)), dma((5,)), dma((count,)), dma,
            each, each, each, each, each, each,
            dma((count,)), dma((count,)), each,
        ],
        compiler_params=pltpu.CompilerParams(
            collective_id=0, has_side_effects=True, vmem_limit_bytes=64 * 1024 * 1024
        ),
        name="mixer",
    )(
        lengths, row_of_segment, signal, filter_taps, out_gate, skip_gain[None, :],
        jnp.asarray(forward), jnp.asarray(inverse),
    )


def on_device(signal, filter_taps, out_gate, skip_gain, lengths, row_of_segment):
    seq_count = lax.axis_size("seq")
    if fits_kernel(signal.shape[0], signal.shape[1], seq_count):
        return fused_on_device(
            seq_count, signal, filter_taps, out_gate, skip_gain, lengths, row_of_segment
        )
    seq_index = lax.axis_index("seq")
    conv = convolve_channels(signal, filter_taps)
    mixed = out_gate * (conv + skip_gain[None, :] * signal)
    pooled = pool_segments(mixed, lengths, row_of_segment, seq_index, seq_count)
    return (mixed, pooled)


def solution(mesh):
    placed = (P("seq", "chan"), P("seq", "chan"), P("seq", "chan"), P("chan"), P(), P())
    return jax.shard_map(
        on_device,
        mesh=mesh,
        in_specs=placed,
        out_specs=(P("seq", "chan"), P("seq", "chan")),
        check_vma=False,
    )
```

```python
import functools
import math

import jax
import jax.numpy as jnp
import ml_dtypes
import numpy as np
from jax import lax
from jax.experimental import pallas as pl
from jax.experimental.pallas import tpu as pltpu
from jax.sharding import PartitionSpec as P

LANES = 128
STORES = 4
MESH = pl.DeviceIdType.MESH

exact_mode = lax.Precision.HIGHEST


def complex_dot(left_re, left_im, right_re, right_im):
    out_re = jnp.dot(left_re, right_re, precision=exact_mode) - jnp.dot(
        left_im, right_im, precision=exact_mode
    )
    out_im = jnp.dot(left_re, right_im, precision=exact_mode) + jnp.dot(
        left_im, right_re, precision=exact_mode
    )
    return (out_re, out_im)


def rotate(real_part, imag_part, phase_angle):
    cosine = jnp.cos(phase_angle)
    sine = jnp.sin(phase_angle)
    return (real_part * cosine - imag_part * sine, real_part * sine + imag_part * cosine)


def local_transform(real_part, imag_part, direction):
    block_rows, columns = real_part.shape
    outer_size = max(
        (divisor for divisor in range(1, math.isqrt(block_rows) + 1) if block_rows % divisor == 0)
    )
    inner_size = block_rows // outer_size
    outer_index = jnp.arange(outer_size, dtype=jnp.int32)
    inner_index = jnp.arange(inner_size, dtype=jnp.int32)
    outer_angle = (
        direction
        * 2.0
        * math.pi
        * (outer_index[:, None] * outer_index[None, :] % outer_size).astype(jnp.float32)
        / outer_size
    )
    twist_angle = (
        direction
        * 2.0
        * math.pi
        * (outer_index[:, None] * inner_index[None, :] % block_rows).astype(jnp.float32)
        / block_rows
    )
    inner_angle = (
        direction
        * 2.0
        * math.pi
        * (inner_index[:, None] * inner_index[None, :] % inner_size).astype(jnp.float32)
        / inner_size
    )
    step_re, step_im = complex_dot(
        jnp.cos(outer_angle),
        jnp.sin(outer_angle),
        real_part.reshape(outer_size, inner_size * columns),
        imag_part.reshape(outer_size, inner_size * columns),
    )
    step_re = step_re.reshape(outer_size, inner_size, columns)
    step_im = step_im.reshape(outer_size, inner_size, columns)
    step_re, step_im = rotate(step_re, step_im, twist_angle[:, :, None])
    inner_cos = jnp.cos(inner_angle)
    inner_sin = jnp.sin(inner_angle)
    out_re = jnp.einsum("sak,at->tsk", step_re, inner_cos, precision=exact_mode) - jnp.einsum(
        "sak,at->tsk", step_im, inner_sin, precision=exact_mode
    )
    out_im = jnp.einsum("sak,at->tsk", step_re, inner_sin, precision=exact_mode) + jnp.einsum(
        "sak,at->tsk", step_im, inner_cos, precision=exact_mode
    )
    return (out_re.reshape(block_rows, columns), out_im.reshape(block_rows, columns))


def convolve_channels(signal, filter_taps):
    signal_cols, taps_cols = (
        lax.all_to_all(signal, "seq", split_axis=1, concat_axis=0, tiled=True),
        lax.all_to_all(filter_taps, "seq", split_axis=1, concat_axis=0, tiled=True),
    )
    total_rows, width = signal_cols.shape
    joined = jnp.concatenate((signal_cols, taps_cols), axis=1)
    padded = jnp.concatenate((joined, jnp.zeros_like(joined)), axis=0)
    spec_re, spec_im = local_transform(padded, jnp.zeros_like(padded), -1.0)
    left_re, left_im = (spec_re[:, :width], spec_im[:, :width])
    right_re, right_im = (spec_re[:, width:], spec_im[:, width:])
    product_re = left_re * right_re - left_im * right_im
    product_im = left_re * right_im + left_im * right_re
    back_re, back_im = local_transform(product_re, product_im, 1.0)
    conv_cols = back_re[:total_rows] / (2.0 * total_rows)
    return lax.all_to_all(conv_cols, "seq", split_axis=0, concat_axis=1, tiled=True)


def pool_segments(mixed, lengths, row_of_segment, seq_index, seq_count):
    block_rows = mixed.shape[0]
    owned_rows = lengths.shape[0] // seq_count
    span_ends = jnp.cumsum(lengths)
    span_starts = span_ends - lengths
    tokens = seq_index * block_rows + jnp.arange(block_rows, dtype=jnp.int32)
    inside = (span_starts[None, :] <= tokens[:, None]) & (tokens[:, None] < span_ends[None, :])
    token_row = jnp.sum(jnp.where(inside, row_of_segment[None, :], 0), axis=1)
    wanted = jnp.arange(owned_rows * lax.axis_size("seq"), dtype=jnp.int32)
    member = (token_row[None, :] == wanted[:, None]).astype(jnp.float32)
    sums = lax.psum_scatter(
        jnp.dot(member, mixed, precision=exact_mode), "seq", scatter_dimension=0, tiled=True
    )
    mine = seq_index * owned_rows + jnp.arange(owned_rows, dtype=jnp.int32)
    seg_sizes = jnp.sum(
        jnp.where(row_of_segment[None, :] == mine[:, None], lengths[None, :], 0), axis=1
    )
    return sums / seg_sizes.astype(jnp.float32)[:, None]


def split_constant(table):
    high = table.astype(np.float32).astype(ml_dtypes.bfloat16)
    low = (table - high.astype(np.float64)).astype(np.float32).astype(ml_dtypes.bfloat16)
    return np.stack([high, low])


def transform_tables(block):
    freqs = np.concatenate([np.arange(0, block, 2), np.arange(1, block, 2)])
    turns = ((2 * freqs[:, None] + 1) * np.arange(block)[None, :]) % (4 * block)
    angle = turns * (np.pi / (2 * block))
    forward = np.concatenate([np.cos(angle), -np.sin(angle)], axis=0)
    inverse = forward.T / block
    return split_constant(forward), split_constant(inverse)


def split_value(value):
    high = value.astype(jnp.bfloat16)
    low = (value - high.astype(jnp.float32)).astype(jnp.bfloat16)
    return high, low


def mul(left, right):
    return jnp.dot(left, right, preferred_element_type=jnp.float32)


def peer_of(me, offset, count):
    peer, place = 0, 1
    while place < count:
        peer = peer + ((me // place + offset // place) % 2) * place
        place *= 2
    return peer


class PeerOf:
    def __init__(self, me, count):
        self.me, self.count = me, count

    def __getitem__(self, offset):
        return peer_of(self.me, offset, self.count)


def mixer_kernel(
    count, block,
    lengths_at, rows_at, signal, taps, gate, skip_at, forward, inverse,
    mixed, pooled,
    sig_in, tap_in, sig_own, gate_own, spec_s, spec_h, prod, acc, conv_out, conv_in, mixed_v, member, part, part_in,
    fwd_v, inv_v, lengths, rows, skip,
    local_sem, table_sem, gate_sem, tap_sem, send_s, recv_s, send_h, recv_h, send_c, recv_c, send_p, recv_p, out_sem,
):
    me = lax.axis_index("seq")
    core = lax.axis_index("chan") % 2
    tokens, width = signal.shape
    lanes = width // count
    halves = tokens // block
    blocks = halves * count
    owned = part.shape[1]
    segs = owned * count
    order = [count - 1 - (e + core) % (count - 1) for e in range(count - 1)]
    peers = PeerOf(me, count)
    pieces = [pl.ds(h * block, block) for h in range(halves)]

    def cols(index):
        return pl.ds(pl.multiple_of(index * lanes, LANES), lanes)

    table_copies = [
        pltpu.make_async_copy(source, target, table_sem.at[i])
        for i, (source, target) in enumerate(
            ((forward, fwd_v), (inverse, inv_v), (lengths_at, lengths), (rows_at, rows), (skip_at, skip))
        )
    ]
    fwd_copy, inv_copy, len_copy, row_copy, skip_copy = table_copies
    tap_copy = pltpu.make_async_copy(taps.at[:, cols(me)], tap_in.at[0], tap_sem)
    sig_copies = [
        pltpu.make_async_copy(signal.at[:, cols(peers[d])], sig_own.at[d], local_sem.at[d]) for d in range(count)
    ]
    gate_copies = [
        pltpu.make_async_copy(gate.at[:, cols(peers[d])], gate_own.at[d], gate_sem.at[d]) for d in range(count)
    ]

    barrier = pltpu.get_barrier_semaphore()
    for d in range(1, count):
        pl.semaphore_signal(barrier, inc=1, device_id={"seq": peers[d]}, device_id_type=MESH)
    fwd_copy.start()
    sig_copies[0].start()
    tap_copy.start()
    len_copy.start()
    row_copy.start()
    pl.semaphore_wait(barrier, count - 1)

    def remote(src, dst, send, recv, peer):
        return pltpu.make_async_remote_copy(
            src_ref=src, dst_ref=dst, send_sem=send, recv_sem=recv,
            device_id={"seq": peer}, device_id_type=MESH,
        )

    def scatter(source, target, send, recv):
        return {
            (e, h): remote(
                source.at[pieces[h], cols(peers[d])], target.at[d, pieces[h], :],
                send.at[d, h], recv.at[d, h], peers[d],
            )
            for h in range(halves)
            for e, d in enumerate(order)
        }

    sig_sends = scatter(signal, sig_in, send_s, recv_s)
    tap_sends = scatter(taps, tap_in, send_h, recv_h)
    for copy in sig_sends.values():
        copy.start()
    inv_copy.start()
    skip_copy.start()
    for d in range(1, count):
        sig_copies[d].start()
    for d in range(count):
        gate_copies[d].start()

    len_copy.wait()
    row_copy.wait()
    token = me * tokens + lax.broadcasted_iota(jnp.int32, (8, tokens), 1)
    mine = me * owned + lax.broadcasted_iota(jnp.int32, (owned, LANES), 0)
    start = jnp.int32(0)
    token_row = jnp.zeros((8, tokens), jnp.int32)
    sizes = jnp.zeros((owned, LANES), jnp.int32)
    for k in range(segs):
        stop = start + lengths[k]
        token_row = jnp.where((token >= start) & (token < stop), rows[k], token_row)
        sizes = jnp.where(mine == rows[k], lengths[k], sizes)
        start = stop
    row_at = lax.broadcasted_iota(jnp.int32, (segs, tokens), 0)
    member[...] = (row_at == token_row[0:1, :]).astype(jnp.float32).astype(jnp.bfloat16)

    fwd_copy.wait()

    def to_spectrum(source, index, spec):
        high, low = split_value(source[...])
        both = mul(fwd_v[0], jnp.concatenate([high, low], axis=1))
        spec[index] = both[:, :lanes] + (both[:, lanes:] + mul(fwd_v[1], high))

    sig_copies[0].wait()
    for h in range(halves):
        to_spectrum(sig_own.at[0, pieces[h], :], me * halves + h, spec_s)
    tap_copy.wait()
    for h in range(halves):
        to_spectrum(tap_in.at[0, pieces[h], :], me * halves + h, spec_h)
    for h in range(halves):
        for e in range(count - 1):
            sig_sends[e, h].wait_recv()
            tap_sends[e, h].start()
        for d in order:
            to_spectrum(sig_in.at[d, pieces[h], :], peers[d] * halves + h, spec_s)

    def take_taps(h):
        for e, d in enumerate(order):
            tap_sends[e, h].wait_recv()
            to_spectrum(tap_in.at[d, pieces[h], :], peers[d] * halves + h, spec_h)

    def load(spec, wanted, re, im):
        return {i: (spec[i, re, :], spec[i, im, :]) for i in wanted}

    def products(first, last, lags, final):
        def tile(sign, row):
            re = pl.ds(pl.multiple_of(row, 8), 8)
            im = pl.ds(pl.multiple_of(row + block, 8), 8)
            used = [k for k in lags if k < last]
            taps_at = load(spec_h, used, re, im)
            sig_at = load(spec_s, sorted({j - k for j in range(first, last) for k in used if k <= j}), re, im)
            old = (acc[first - 1, re, :], acc[first - 1, im, :]) if final and first else None
            for j in range(first, last):
                total = (acc[j, re, :], acc[j, im, :]) if final else None
                for k in used:
                    if k <= j:
                        (a, b), (c, d) = sig_at[j - k], taps_at[k]
                        new = (a * c - b * d, a * d + b * c)
                        total = new if total is None else (total[0] + new[0], total[1] + new[1])
                if not final:
                    acc[j, re, :], acc[j, im, :] = total
                    continue
                out = total
                if j:
                    out = (total[0] - sign * old[1], total[1] + sign * old[0])
                at = pl.ds((j % halves) * lanes, lanes)
                prod[j // halves, re, at], prod[j // halves, im, at] = out
                old = total
            if final and last < blocks:
                acc[last - 1, re, :], acc[last - 1, im, :] = old

        for sign, base in ((1, 0), (-1, block // 2)):
            def body(t, state, sign=sign, base=base):
                tile(sign, base + t * 8)
                return state
            lax.fori_loop(0, block // 16, body, 0)

    for h in range(halves - 1):
        take_taps(h)
    products(0, blocks, [k for k in range(blocks) if k % halves < halves - 1], False)
    take_taps(halves - 1)
    late_lags = [k for k in range(blocks) if k % halves == halves - 1]

    def back_copy(d, h, peer):
        return remote(
            conv_out.at[d, pieces[h], :], conv_in.at[d, pieces[h], :], send_c.at[d, h], recv_c.at[d, h], peer
        )

    def give_back(owner):
        high, low = split_value(prod[owner])
        result = mul(inv_v[0], high) + (mul(inv_v[1], high) + mul(inv_v[0], low))
        d = peer_of(me, owner, count)
        for h in range(halves):
            conv_out[d, pieces[h], :] = result[:, h * lanes:(h + 1) * lanes]

        @pl.when(me != owner)
        def _():
            for h in range(halves):
                back_copy(d, h, owner).start()

    inv_copy.wait()
    products(0, blocks // 2, late_lags, True)
    for owner in range(count // 2):
        give_back(owner)
    products(blocks // 2, blocks, late_lags, True)
    for owner in range(count // 2, count):
        give_back(owner)

    out_copies = []

    def finish(d, h, conv):
        at = cols(peers[d])
        value = gate_own[d, pieces[h], :] * (conv[d, pieces[h], :] + skip[:, at] * sig_own[d, pieces[h], :])
        mixed_v[d, pieces[h], :] = value
        copy = pltpu.make_async_copy(mixed_v.at[d, pieces[h], :], mixed.at[pieces[h], at], out_sem.at[d, h])
        copy.start()
        out_copies.append(copy)
        high, low = split_value(value)
        inside = member[:, h * block:(h + 1) * block]
        sums = mul(inside, high) + mul(inside, low)
        for p in range(count):
            new = sums[p * owned:(p + 1) * owned]
            part[p, :, at] = part[p, :, at] + new if h else new

    skip_copy.wait()
    for d in range(count):
        if d:
            sig_copies[d].wait()
        gate_copies[d].wait()
        for h in range(halves):
            if d:
                back_copy(d, h, peers[d]).wait_recv()
            finish(d, h, conv_in if d else conv_out)

    part_sends = [
        remote(part.at[peers[d]], part_in.at[d], send_p.at[d], recv_p.at[d], peers[d]) for d in order
    ]
    for copy in part_sends:
        copy.start()
    total = part[me]
    for d, copy in zip(order, part_sends):
        copy.wait_recv()
        total = total + part_in[d]
    pooled[...] = total / jnp.concatenate([sizes] * (width // LANES), axis=1).astype(jnp.float32)

    for copy in out_copies:
        copy.wait()
    for copy in [*sig_sends.values(), *tap_sends.values(), *part_sends]:
        copy.wait_send()
    for d in order:
        for h in range(halves):
            back_copy(d, h, peers[d]).wait_send()


def store_kernel(mixed_v, pooled_v, mixed, pooled, sem):
    rows = mixed.shape[0] // STORES
    parts = [pl.ds(i * rows, rows) for i in range(STORES)]
    copies = [pltpu.make_async_copy(mixed_v.at[at, :], mixed.at[at, :], sem.at[i]) for i, at in enumerate(parts)]
    copies.append(pltpu.make_async_copy(pooled_v, pooled, sem.at[STORES]))
    for copy in copies:
        copy.start()
    for copy in copies:
        copy.wait()


def fits_kernel(tokens, width, count):
    return (
        count > 1
        and count & (count - 1) == 0
        and width % (count * LANES) == 0
        and tokens % (4 * LANES) == 0
    )


def fused_on_device(count, signal, filter_taps, out_gate, skip_gain, lengths, row_of_segment):
    tokens, width = signal.shape
    lanes = width // count
    block = 2 * LANES
    halves = tokens // block
    owned = lengths.shape[0] // count
    segs = owned * count
    forward, inverse = transform_tables(block)
    f32, bf16 = jnp.float32, jnp.bfloat16
    dma = pltpu.SemaphoreType.DMA
    each = dma((count, halves))
    anywhere = pl.BlockSpec(memory_space=pl.ANY)
    vmem = pl.BlockSpec(memory_space=pltpu.VMEM)
    piece = pltpu.VMEM((count, tokens, lanes), f32)
    spectra = pltpu.VMEM((count * halves, 2 * block, lanes), f32)
    results = pl.pallas_call(
        functools.partial(mixer_kernel, count, block),
        out_shape=(
            pltpu.VMEM((tokens, width), f32),
            pltpu.VMEM((owned, width), f32),
        ),
        in_specs=[anywhere] * 8,
        out_specs=(anywhere, vmem),
        scratch_shapes=[
            piece, piece, piece, piece, spectra, spectra,
            pltpu.VMEM((count, 2 * block, halves * lanes), f32),
            spectra,
            piece, piece, piece,
            pltpu.VMEM((segs, tokens), bf16),
            pltpu.VMEM((count, owned, width), f32),
            pltpu.VMEM((count, owned, width), f32),
            pltpu.VMEM(forward.shape, bf16),
            pltpu.VMEM(inverse.shape, bf16),
            pltpu.SMEM(lengths.shape, jnp.int32),
            pltpu.SMEM(lengths.shape, jnp.int32),
            pltpu.VMEM((1, width), f32),
            dma((count,)), dma((5,)), dma((count,)), dma,
            each, each, each, each, each, each,
            dma((count,)), dma((count,)), each,
        ],
        compiler_params=pltpu.CompilerParams(
            collective_id=0, has_side_effects=True, vmem_limit_bytes=62 * 1024 * 1024
        ),
        name="mixer",
    )(
        lengths, row_of_segment, signal, filter_taps, out_gate, skip_gain[None, :],
        jnp.asarray(forward), jnp.asarray(inverse),
    )
    return pl.pallas_call(
        store_kernel,
        out_shape=tuple(pltpu.HBM(result.shape, f32) for result in results),
        in_specs=[anywhere] * 2,
        out_specs=(anywhere,) * 2,
        scratch_shapes=[dma((STORES + 1,))],
        compiler_params=pltpu.CompilerParams(vmem_limit_bytes=1024 * 1024),
        name="store",
    )(*results)


def on_device(signal, filter_taps, out_gate, skip_gain, lengths, row_of_segment):
    seq_count = lax.axis_size("seq")
    if fits_kernel(signal.shape[0], signal.shape[1], seq_count):
        return fused_on_device(
            seq_count, signal, filter_taps, out_gate, skip_gain, lengths, row_of_segment
        )
    seq_index = lax.axis_index("seq")
    conv = convolve_channels(signal, filter_taps)
    mixed = out_gate * (conv + skip_gain[None, :] * signal)
    pooled = pool_segments(mixed, lengths, row_of_segment, seq_index, seq_count)
    return (mixed, pooled)


def solution(mesh):
    placed = (P("seq", "chan"), P("seq", "chan"), P("seq", "chan"), P("chan"), P(), P())
    return jax.shard_map(
        on_device,
        mesh=mesh,
        in_specs=placed,
        out_specs=(P("seq", "chan"), P("seq", "chan")),
        check_vma=False,
    )
```

```python
import functools
import math

import jax
import jax.numpy as jnp
import ml_dtypes
import numpy as np
from jax import lax
from jax.experimental import pallas as pl
from jax.experimental.pallas import tpu as pltpu
from jax.sharding import PartitionSpec as P

LANES = 128
STORES = 4
MESH = pl.DeviceIdType.MESH

exact_mode = lax.Precision.HIGHEST


def complex_dot(left_re, left_im, right_re, right_im):
    out_re = jnp.dot(left_re, right_re, precision=exact_mode) - jnp.dot(
        left_im, right_im, precision=exact_mode
    )
    out_im = jnp.dot(left_re, right_im, precision=exact_mode) + jnp.dot(
        left_im, right_re, precision=exact_mode
    )
    return (out_re, out_im)


def rotate(real_part, imag_part, phase_angle):
    cosine = jnp.cos(phase_angle)
    sine = jnp.sin(phase_angle)
    return (real_part * cosine - imag_part * sine, real_part * sine + imag_part * cosine)


def local_transform(real_part, imag_part, direction):
    block_rows, columns = real_part.shape
    outer_size = max(
        (divisor for divisor in range(1, math.isqrt(block_rows) + 1) if block_rows % divisor == 0)
    )
    inner_size = block_rows // outer_size
    outer_index = jnp.arange(outer_size, dtype=jnp.int32)
    inner_index = jnp.arange(inner_size, dtype=jnp.int32)
    outer_angle = (
        direction
        * 2.0
        * math.pi
        * (outer_index[:, None] * outer_index[None, :] % outer_size).astype(jnp.float32)
        / outer_size
    )
    twist_angle = (
        direction
        * 2.0
        * math.pi
        * (outer_index[:, None] * inner_index[None, :] % block_rows).astype(jnp.float32)
        / block_rows
    )
    inner_angle = (
        direction
        * 2.0
        * math.pi
        * (inner_index[:, None] * inner_index[None, :] % inner_size).astype(jnp.float32)
        / inner_size
    )
    step_re, step_im = complex_dot(
        jnp.cos(outer_angle),
        jnp.sin(outer_angle),
        real_part.reshape(outer_size, inner_size * columns),
        imag_part.reshape(outer_size, inner_size * columns),
    )
    step_re = step_re.reshape(outer_size, inner_size, columns)
    step_im = step_im.reshape(outer_size, inner_size, columns)
    step_re, step_im = rotate(step_re, step_im, twist_angle[:, :, None])
    inner_cos = jnp.cos(inner_angle)
    inner_sin = jnp.sin(inner_angle)
    out_re = jnp.einsum("sak,at->tsk", step_re, inner_cos, precision=exact_mode) - jnp.einsum(
        "sak,at->tsk", step_im, inner_sin, precision=exact_mode
    )
    out_im = jnp.einsum("sak,at->tsk", step_re, inner_sin, precision=exact_mode) + jnp.einsum(
        "sak,at->tsk", step_im, inner_cos, precision=exact_mode
    )
    return (out_re.reshape(block_rows, columns), out_im.reshape(block_rows, columns))


def convolve_channels(signal, filter_taps):
    signal_cols, taps_cols = (
        lax.all_to_all(signal, "seq", split_axis=1, concat_axis=0, tiled=True),
        lax.all_to_all(filter_taps, "seq", split_axis=1, concat_axis=0, tiled=True),
    )
    total_rows, width = signal_cols.shape
    joined = jnp.concatenate((signal_cols, taps_cols), axis=1)
    padded = jnp.concatenate((joined, jnp.zeros_like(joined)), axis=0)
    spec_re, spec_im = local_transform(padded, jnp.zeros_like(padded), -1.0)
    left_re, left_im = (spec_re[:, :width], spec_im[:, :width])
    right_re, right_im = (spec_re[:, width:], spec_im[:, width:])
    product_re = left_re * right_re - left_im * right_im
    product_im = left_re * right_im + left_im * right_re
    back_re, back_im = local_transform(product_re, product_im, 1.0)
    conv_cols = back_re[:total_rows] / (2.0 * total_rows)
    return lax.all_to_all(conv_cols, "seq", split_axis=0, concat_axis=1, tiled=True)


def pool_segments(mixed, lengths, row_of_segment, seq_index, seq_count):
    block_rows = mixed.shape[0]
    owned_rows = lengths.shape[0] // seq_count
    span_ends = jnp.cumsum(lengths)
    span_starts = span_ends - lengths
    tokens = seq_index * block_rows + jnp.arange(block_rows, dtype=jnp.int32)
    inside = (span_starts[None, :] <= tokens[:, None]) & (tokens[:, None] < span_ends[None, :])
    token_row = jnp.sum(jnp.where(inside, row_of_segment[None, :], 0), axis=1)
    wanted = jnp.arange(owned_rows * lax.axis_size("seq"), dtype=jnp.int32)
    member = (token_row[None, :] == wanted[:, None]).astype(jnp.float32)
    sums = lax.psum_scatter(
        jnp.dot(member, mixed, precision=exact_mode), "seq", scatter_dimension=0, tiled=True
    )
    mine = seq_index * owned_rows + jnp.arange(owned_rows, dtype=jnp.int32)
    seg_sizes = jnp.sum(
        jnp.where(row_of_segment[None, :] == mine[:, None], lengths[None, :], 0), axis=1
    )
    return sums / seg_sizes.astype(jnp.float32)[:, None]


def split_constant(table):
    high = table.astype(np.float32).astype(ml_dtypes.bfloat16)
    low = (table - high.astype(np.float64)).astype(np.float32).astype(ml_dtypes.bfloat16)
    return np.stack([high, low])


def transform_tables(block):
    freqs = np.concatenate([np.arange(0, block, 2), np.arange(1, block, 2)])
    turns = ((2 * freqs[:, None] + 1) * np.arange(block)[None, :]) % (4 * block)
    angle = turns * (np.pi / (2 * block))
    forward = np.concatenate([np.cos(angle), -np.sin(angle)], axis=0)
    inverse = forward.T / block
    return split_constant(forward), split_constant(inverse)


def split_value(value):
    high = value.astype(jnp.bfloat16)
    low = (value - high.astype(jnp.float32)).astype(jnp.bfloat16)
    return high, low


def mul(left, right):
    return jnp.dot(left, right, preferred_element_type=jnp.float32)


def peer_of(me, offset, count):
    peer, place = 0, 1
    while place < count:
        peer = peer + ((me // place + offset // place) % 2) * place
        place *= 2
    return peer


class PeerOf:
    def __init__(self, me, count):
        self.me, self.count = me, count

    def __getitem__(self, offset):
        return peer_of(self.me, offset, self.count)


def mixer_kernel(
    count, block,
    lengths_at, rows_at, signal, taps, gate, skip_at, forward, inverse,
    mixed, pooled,
    sig_in, tap_in, sig_own, gate_own, spec_s, spec_h, prod, acc, conv_out, conv_in, mixed_v, member, part, part_in,
    fwd_v, inv_v, lengths, rows, skip,
    local_sem, table_sem, gate_sem, tap_sem, send_s, recv_s, send_h, recv_h, send_c, recv_c, send_p, recv_p, out_sem,
):
    me = lax.axis_index("seq")
    core = lax.axis_index("chan") % 2
    tokens, width = signal.shape
    lanes = width // count
    halves = tokens // block
    blocks = halves * count
    owned = part.shape[1]
    segs = owned * count
    order = [count - 1] + [1 + (e + core) % (count - 2) for e in range(count - 2)]
    peers = PeerOf(me, count)
    pieces = [pl.ds(h * block, block) for h in range(halves)]

    def cols(index):
        return pl.ds(pl.multiple_of(index * lanes, LANES), lanes)

    table_copies = [
        pltpu.make_async_copy(source, target, table_sem.at[i])
        for i, (source, target) in enumerate(
            ((forward, fwd_v), (inverse, inv_v), (lengths_at, lengths), (rows_at, rows), (skip_at, skip))
        )
    ]
    fwd_copy, inv_copy, len_copy, row_copy, skip_copy = table_copies
    tap_copy = pltpu.make_async_copy(taps.at[:, cols(me)], tap_in.at[0], tap_sem)
    sig_copies = [
        pltpu.make_async_copy(signal.at[:, cols(peers[d])], sig_own.at[d], local_sem.at[d]) for d in range(count)
    ]
    gate_copies = [
        pltpu.make_async_copy(gate.at[:, cols(peers[d])], gate_own.at[d], gate_sem.at[d]) for d in range(count)
    ]

    barrier = pltpu.get_barrier_semaphore()
    for d in range(1, count):
        pl.semaphore_signal(barrier, inc=1, device_id={"seq": peers[d]}, device_id_type=MESH)
    fwd_copy.start()
    sig_copies[0].start()
    tap_copy.start()
    len_copy.start()
    row_copy.start()
    pl.semaphore_wait(barrier, count - 1)

    def remote(src, dst, send, recv, peer):
        return pltpu.make_async_remote_copy(
            src_ref=src, dst_ref=dst, send_sem=send, recv_sem=recv,
            device_id={"seq": peer}, device_id_type=MESH,
        )

    def scatter(source, target, send, recv):
        return {
            (e, h): remote(
                source.at[pieces[h], cols(peers[d])], target.at[d, pieces[h], :],
                send.at[d, h], recv.at[d, h], peers[d],
            )
            for h in range(halves)
            for e, d in enumerate(order)
        }

    sig_sends = scatter(signal, sig_in, send_s, recv_s)
    tap_sends = scatter(taps, tap_in, send_h, recv_h)
    for copy in sig_sends.values():
        copy.start()
    inv_copy.start()
    skip_copy.start()
    for d in range(1, count):
        sig_copies[d].start()
    for d in range(count):
        gate_copies[d].start()

    len_copy.wait()
    row_copy.wait()
    token = me * tokens + lax.broadcasted_iota(jnp.int32, (8, tokens), 1)
    mine = me * owned + lax.broadcasted_iota(jnp.int32, (owned, LANES), 0)
    start = jnp.int32(0)
    token_row = jnp.zeros((8, tokens), jnp.int32)
    sizes = jnp.zeros((owned, LANES), jnp.int32)
    for k in range(segs):
        stop = start + lengths[k]
        token_row = jnp.where((token >= start) & (token < stop), rows[k], token_row)
        sizes = jnp.where(mine == rows[k], lengths[k], sizes)
        start = stop
    row_at = lax.broadcasted_iota(jnp.int32, (segs, tokens), 0)
    member[...] = (row_at == token_row[0:1, :]).astype(jnp.float32).astype(jnp.bfloat16)

    fwd_copy.wait()

    def to_spectrum(source, index, spec):
        high, low = split_value(source[...])
        both = mul(fwd_v[0], jnp.concatenate([high, low], axis=1))
        spec[index] = both[:, :lanes] + (both[:, lanes:] + mul(fwd_v[1], high))

    sig_copies[0].wait()
    for h in range(halves):
        to_spectrum(sig_own.at[0, pieces[h], :], me * halves + h, spec_s)
    tap_copy.wait()
    for h in range(halves):
        to_spectrum(tap_in.at[0, pieces[h], :], me * halves + h, spec_h)
    for h in range(halves):
        for e in range(count - 1):
            sig_sends[e, h].wait_recv()
            tap_sends[e, h].start()
        for d in order:
            to_spectrum(sig_in.at[d, pieces[h], :], peers[d] * halves + h, spec_s)

    def take_taps(h):
        for e, d in enumerate(order):
            tap_sends[e, h].wait_recv()
            to_spectrum(tap_in.at[d, pieces[h], :], peers[d] * halves + h, spec_h)

    def load(spec, wanted, re, im):
        return {i: (spec[i, re, :], spec[i, im, :]) for i in wanted}

    def products(first, last, lags, final):
        def tile(sign, row):
            re = pl.ds(pl.multiple_of(row, 8), 8)
            im = pl.ds(pl.multiple_of(row + block, 8), 8)
            used = [k for k in lags if k < last]
            taps_at = load(spec_h, used, re, im)
            sig_at = load(spec_s, sorted({j - k for j in range(first, last) for k in used if k <= j}), re, im)
            old = (acc[first - 1, re, :], acc[first - 1, im, :]) if final and first else None
            for j in range(first, last):
                total = (acc[j, re, :], acc[j, im, :]) if final else None
                for k in used:
                    if k <= j:
                        (a, b), (c, d) = sig_at[j - k], taps_at[k]
                        new = (a * c - b * d, a * d + b * c)
                        total = new if total is None else (total[0] + new[0], total[1] + new[1])
                if not final:
                    acc[j, re, :], acc[j, im, :] = total
                    continue
                out = total
                if j:
                    out = (total[0] - sign * old[1], total[1] + sign * old[0])
                at = pl.ds((j % halves) * lanes, lanes)
                prod[j // halves, re, at], prod[j // halves, im, at] = out
                old = total
            if final and last < blocks:
                acc[last - 1, re, :], acc[last - 1, im, :] = old

        for sign, base in ((1, 0), (-1, block // 2)):
            def body(t, state, sign=sign, base=base):
                tile(sign, base + t * 8)
                return state
            lax.fori_loop(0, block // 16, body, 0)

    for h in range(halves - 1):
        take_taps(h)
    products(0, blocks, [k for k in range(blocks) if k % halves < halves - 1], False)
    take_taps(halves - 1)
    late_lags = [k for k in range(blocks) if k % halves == halves - 1]

    def back_copy(d, h, peer):
        return remote(
            conv_out.at[d, pieces[h], :], conv_in.at[d, pieces[h], :], send_c.at[d, h], recv_c.at[d, h], peer
        )

    def give_back(d):
        high, low = split_value(prod[peers[d]])
        result = mul(inv_v[0], high) + (mul(inv_v[1], high) + mul(inv_v[0], low))
        for h in range(halves):
            conv_out[d, pieces[h], :] = result[:, h * lanes:(h + 1) * lanes]

    inv_copy.wait()
    products(0, blocks, late_lags, True)
    for d in order:
        give_back(d)
        for h in range(halves):
            back_copy(d, h, peers[d]).start()
    give_back(0)

    out_copies = []

    def finish(d, h, conv):
        at = cols(peers[d])
        value = gate_own[d, pieces[h], :] * (conv[d, pieces[h], :] + skip[:, at] * sig_own[d, pieces[h], :])
        mixed_v[d, pieces[h], :] = value
        copy = pltpu.make_async_copy(mixed_v.at[d, pieces[h], :], mixed.at[pieces[h], at], out_sem.at[d, h])
        copy.start()
        out_copies.append(copy)
        high, low = split_value(value)
        inside = member[:, h * block:(h + 1) * block]
        sums = mul(inside, high) + mul(inside, low)
        for p in range(count):
            new = sums[p * owned:(p + 1) * owned]
            part[p, :, at] = part[p, :, at] + new if h else new

    skip_copy.wait()
    for d in range(count):
        if d:
            sig_copies[d].wait()
        gate_copies[d].wait()
    for h in range(halves):
        finish(0, h, conv_out)
    for d in order:
        for h in range(halves):
            back_copy(d, h, peers[d]).wait_recv()
            finish(d, h, conv_in)

    part_sends = [
        remote(part.at[peers[d]], part_in.at[d], send_p.at[d], recv_p.at[d], peers[d]) for d in order
    ]
    for copy in part_sends:
        copy.start()
    total = part[me]
    for d, copy in zip(order, part_sends):
        copy.wait_recv()
        total = total + part_in[d]
    pooled[...] = total / jnp.concatenate([sizes] * (width // LANES), axis=1).astype(jnp.float32)

    for copy in out_copies:
        copy.wait()
    for copy in [*sig_sends.values(), *tap_sends.values(), *part_sends]:
        copy.wait_send()
    for d in order:
        for h in range(halves):
            back_copy(d, h, peers[d]).wait_send()


def store_kernel(mixed_v, pooled_v, mixed, pooled, sem):
    rows = mixed.shape[0] // STORES
    parts = [pl.ds(i * rows, rows) for i in range(STORES)]
    copies = [pltpu.make_async_copy(mixed_v.at[at, :], mixed.at[at, :], sem.at[i]) for i, at in enumerate(parts)]
    copies.append(pltpu.make_async_copy(pooled_v, pooled, sem.at[STORES]))
    for copy in copies:
        copy.start()
    for copy in copies:
        copy.wait()


def fits_kernel(tokens, width, count):
    return (
        count > 1
        and count & (count - 1) == 0
        and width % (count * LANES) == 0
        and tokens % (4 * LANES) == 0
    )


def fused_on_device(count, signal, filter_taps, out_gate, skip_gain, lengths, row_of_segment):
    tokens, width = signal.shape
    lanes = width // count
    block = 2 * LANES
    halves = tokens // block
    owned = lengths.shape[0] // count
    segs = owned * count
    forward, inverse = transform_tables(block)
    f32, bf16 = jnp.float32, jnp.bfloat16
    dma = pltpu.SemaphoreType.DMA
    each = dma((count, halves))
    anywhere = pl.BlockSpec(memory_space=pl.ANY)
    vmem = pl.BlockSpec(memory_space=pltpu.VMEM)
    piece = pltpu.VMEM((count, tokens, lanes), f32)
    spectra = pltpu.VMEM((count * halves, 2 * block, lanes), f32)
    results = pl.pallas_call(
        functools.partial(mixer_kernel, count, block),
        out_shape=(
            pltpu.VMEM((tokens, width), f32),
            pltpu.VMEM((owned, width), f32),
        ),
        in_specs=[anywhere] * 8,
        out_specs=(anywhere, vmem),
        scratch_shapes=[
            piece, piece, piece, piece, spectra, spectra,
            pltpu.VMEM((count, 2 * block, halves * lanes), f32),
            spectra,
            piece, piece, piece,
            pltpu.VMEM((segs, tokens), bf16),
            pltpu.VMEM((count, owned, width), f32),
            pltpu.VMEM((count, owned, width), f32),
            pltpu.VMEM(forward.shape, bf16),
            pltpu.VMEM(inverse.shape, bf16),
            pltpu.SMEM(lengths.shape, jnp.int32),
            pltpu.SMEM(lengths.shape, jnp.int32),
            pltpu.VMEM((1, width), f32),
            dma((count,)), dma((5,)), dma((count,)), dma,
            each, each, each, each, each, each,
            dma((count,)), dma((count,)), each,
        ],
        compiler_params=pltpu.CompilerParams(
            collective_id=0, has_side_effects=True, vmem_limit_bytes=62 * 1024 * 1024
        ),
        name="mixer",
    )(
        lengths, row_of_segment, signal, filter_taps, out_gate, skip_gain[None, :],
        jnp.asarray(forward), jnp.asarray(inverse),
    )
    return pl.pallas_call(
        store_kernel,
        out_shape=tuple(pltpu.HBM(result.shape, f32) for result in results),
        in_specs=[anywhere] * 2,
        out_specs=(anywhere,) * 2,
        scratch_shapes=[dma((STORES + 1,))],
        compiler_params=pltpu.CompilerParams(vmem_limit_bytes=1024 * 1024),
        name="store",
    )(*results)


def on_device(signal, filter_taps, out_gate, skip_gain, lengths, row_of_segment):
    seq_count = lax.axis_size("seq")
    if fits_kernel(signal.shape[0], signal.shape[1], seq_count):
        return fused_on_device(
            seq_count, signal, filter_taps, out_gate, skip_gain, lengths, row_of_segment
        )
    seq_index = lax.axis_index("seq")
    conv = convolve_channels(signal, filter_taps)
    mixed = out_gate * (conv + skip_gain[None, :] * signal)
    pooled = pool_segments(mixed, lengths, row_of_segment, seq_index, seq_count)
    return (mixed, pooled)


def solution(mesh):
    placed = (P("seq", "chan"), P("seq", "chan"), P("seq", "chan"), P("chan"), P(), P())
    return jax.shard_map(
        on_device,
        mesh=mesh,
        in_specs=placed,
        out_specs=(P("seq", "chan"), P("seq", "chan")),
        check_vma=False,
    )
```

```python
import functools
import math

import jax
import jax.numpy as jnp
import ml_dtypes
import numpy as np
from jax import lax
from jax.experimental import pallas as pl
from jax.experimental.pallas import tpu as pltpu
from jax.sharding import PartitionSpec as P

LANES = 128
STORES = 4
MESH = pl.DeviceIdType.MESH

exact_mode = lax.Precision.HIGHEST


def complex_dot(left_re, left_im, right_re, right_im):
    out_re = jnp.dot(left_re, right_re, precision=exact_mode) - jnp.dot(
        left_im, right_im, precision=exact_mode
    )
    out_im = jnp.dot(left_re, right_im, precision=exact_mode) + jnp.dot(
        left_im, right_re, precision=exact_mode
    )
    return (out_re, out_im)


def rotate(real_part, imag_part, phase_angle):
    cosine = jnp.cos(phase_angle)
    sine = jnp.sin(phase_angle)
    return (real_part * cosine - imag_part * sine, real_part * sine + imag_part * cosine)


def local_transform(real_part, imag_part, direction):
    block_rows, columns = real_part.shape
    outer_size = max(
        (divisor for divisor in range(1, math.isqrt(block_rows) + 1) if block_rows % divisor == 0)
    )
    inner_size = block_rows // outer_size
    outer_index = jnp.arange(outer_size, dtype=jnp.int32)
    inner_index = jnp.arange(inner_size, dtype=jnp.int32)
    outer_angle = (
        direction
        * 2.0
        * math.pi
        * (outer_index[:, None] * outer_index[None, :] % outer_size).astype(jnp.float32)
        / outer_size
    )
    twist_angle = (
        direction
        * 2.0
        * math.pi
        * (outer_index[:, None] * inner_index[None, :] % block_rows).astype(jnp.float32)
        / block_rows
    )
    inner_angle = (
        direction
        * 2.0
        * math.pi
        * (inner_index[:, None] * inner_index[None, :] % inner_size).astype(jnp.float32)
        / inner_size
    )
    step_re, step_im = complex_dot(
        jnp.cos(outer_angle),
        jnp.sin(outer_angle),
        real_part.reshape(outer_size, inner_size * columns),
        imag_part.reshape(outer_size, inner_size * columns),
    )
    step_re = step_re.reshape(outer_size, inner_size, columns)
    step_im = step_im.reshape(outer_size, inner_size, columns)
    step_re, step_im = rotate(step_re, step_im, twist_angle[:, :, None])
    inner_cos = jnp.cos(inner_angle)
    inner_sin = jnp.sin(inner_angle)
    out_re = jnp.einsum("sak,at->tsk", step_re, inner_cos, precision=exact_mode) - jnp.einsum(
        "sak,at->tsk", step_im, inner_sin, precision=exact_mode
    )
    out_im = jnp.einsum("sak,at->tsk", step_re, inner_sin, precision=exact_mode) + jnp.einsum(
        "sak,at->tsk", step_im, inner_cos, precision=exact_mode
    )
    return (out_re.reshape(block_rows, columns), out_im.reshape(block_rows, columns))


def convolve_channels(signal, filter_taps):
    signal_cols, taps_cols = (
        lax.all_to_all(signal, "seq", split_axis=1, concat_axis=0, tiled=True),
        lax.all_to_all(filter_taps, "seq", split_axis=1, concat_axis=0, tiled=True),
    )
    total_rows, width = signal_cols.shape
    joined = jnp.concatenate((signal_cols, taps_cols), axis=1)
    padded = jnp.concatenate((joined, jnp.zeros_like(joined)), axis=0)
    spec_re, spec_im = local_transform(padded, jnp.zeros_like(padded), -1.0)
    left_re, left_im = (spec_re[:, :width], spec_im[:, :width])
    right_re, right_im = (spec_re[:, width:], spec_im[:, width:])
    product_re = left_re * right_re - left_im * right_im
    product_im = left_re * right_im + left_im * right_re
    back_re, back_im = local_transform(product_re, product_im, 1.0)
    conv_cols = back_re[:total_rows] / (2.0 * total_rows)
    return lax.all_to_all(conv_cols, "seq", split_axis=0, concat_axis=1, tiled=True)


def pool_segments(mixed, lengths, row_of_segment, seq_index, seq_count):
    block_rows = mixed.shape[0]
    owned_rows = lengths.shape[0] // seq_count
    span_ends = jnp.cumsum(lengths)
    span_starts = span_ends - lengths
    tokens = seq_index * block_rows + jnp.arange(block_rows, dtype=jnp.int32)
    inside = (span_starts[None, :] <= tokens[:, None]) & (tokens[:, None] < span_ends[None, :])
    token_row = jnp.sum(jnp.where(inside, row_of_segment[None, :], 0), axis=1)
    wanted = jnp.arange(owned_rows * lax.axis_size("seq"), dtype=jnp.int32)
    member = (token_row[None, :] == wanted[:, None]).astype(jnp.float32)
    sums = lax.psum_scatter(
        jnp.dot(member, mixed, precision=exact_mode), "seq", scatter_dimension=0, tiled=True
    )
    mine = seq_index * owned_rows + jnp.arange(owned_rows, dtype=jnp.int32)
    seg_sizes = jnp.sum(
        jnp.where(row_of_segment[None, :] == mine[:, None], lengths[None, :], 0), axis=1
    )
    return sums / seg_sizes.astype(jnp.float32)[:, None]


def split_constant(table):
    high = table.astype(np.float32).astype(ml_dtypes.bfloat16)
    low = (table - high.astype(np.float64)).astype(np.float32).astype(ml_dtypes.bfloat16)
    return np.stack([high, low])


def transform_tables(block):
    freqs = np.concatenate([np.arange(0, block, 2), np.arange(1, block, 2)])
    turns = ((2 * freqs[:, None] + 1) * np.arange(block)[None, :]) % (4 * block)
    angle = turns * (np.pi / (2 * block))
    forward = np.concatenate([np.cos(angle), -np.sin(angle)], axis=0)
    inverse = forward.T / block
    return split_constant(forward), split_constant(inverse)


def split_value(value):
    high = value.astype(jnp.bfloat16)
    low = (value - high.astype(jnp.float32)).astype(jnp.bfloat16)
    return high, low


def mul(left, right):
    return jnp.dot(left, right, preferred_element_type=jnp.float32)


def peer_of(me, offset, count):
    peer, place = 0, 1
    while place < count:
        peer = peer + ((me // place + offset // place) % 2) * place
        place *= 2
    return peer


class PeerOf:
    def __init__(self, me, count):
        self.me, self.count = me, count

    def __getitem__(self, offset):
        return peer_of(self.me, offset, self.count)


def mixer_kernel(
    count, block,
    lengths_at, rows_at, signal, taps, gate, skip_at, forward, inverse,
    mixed, pooled,
    sig_in, tap_in, sig_own, gate_own, spec_s, spec_h, prod, acc, conv_out, conv_in, mixed_v, member, part, part_in,
    fwd_v, inv_v, lengths, rows, skip,
    local_sem, table_sem, gate_sem, tap_sem, send_s, recv_s, send_h, recv_h, send_c, recv_c, send_p, recv_p, out_sem,
):
    me = lax.axis_index("seq")
    core = lax.axis_index("chan") % 2
    tokens, width = signal.shape
    lanes = width // count
    halves = tokens // block
    blocks = halves * count
    owned = part.shape[1]
    segs = owned * count
    order = [count - 1] + [1 + (e + core) % (count - 2) for e in range(count - 2)]
    peers = PeerOf(me, count)
    pieces = [pl.ds(h * block, block) for h in range(halves)]

    def cols(index):
        return pl.ds(pl.multiple_of(index * lanes, LANES), lanes)

    table_copies = [
        pltpu.make_async_copy(source, target, table_sem.at[i])
        for i, (source, target) in enumerate(
            ((forward, fwd_v), (inverse, inv_v), (lengths_at, lengths), (rows_at, rows), (skip_at, skip))
        )
    ]
    fwd_copy, inv_copy, len_copy, row_copy, skip_copy = table_copies
    tap_copy = pltpu.make_async_copy(taps.at[:, cols(me)], tap_in.at[0], tap_sem)
    sig_copies = [
        pltpu.make_async_copy(signal.at[:, cols(peers[d])], sig_own.at[d], local_sem.at[d]) for d in range(count)
    ]
    gate_copies = [
        pltpu.make_async_copy(gate.at[:, cols(peers[d])], gate_own.at[d], gate_sem.at[d]) for d in range(count)
    ]

    barrier = pltpu.get_barrier_semaphore()
    for d in range(1, count):
        pl.semaphore_signal(barrier, inc=1, device_id={"seq": peers[d]}, device_id_type=MESH)
    fwd_copy.start()
    sig_copies[0].start()
    tap_copy.start()
    len_copy.start()
    row_copy.start()
    pl.semaphore_wait(barrier, count - 1)

    def remote(src, dst, send, recv, peer):
        return pltpu.make_async_remote_copy(
            src_ref=src, dst_ref=dst, send_sem=send, recv_sem=recv,
            device_id={"seq": peer}, device_id_type=MESH,
        )

    def scatter(source, target, send, recv):
        return {
            (e, h): remote(
                source.at[pieces[h], cols(peers[d])], target.at[d, pieces[h], :],
                send.at[d, h], recv.at[d, h], peers[d],
            )
            for h in range(halves)
            for e, d in enumerate(order)
        }

    sig_sends = scatter(signal, sig_in, send_s, recv_s)
    tap_sends = scatter(taps, tap_in, send_h, recv_h)
    for copy in sig_sends.values():
        copy.start()
    for e in range(count - 1):
        tap_sends[e, 0].start()
    inv_copy.start()
    skip_copy.start()
    for d in range(1, count):
        sig_copies[d].start()
    for d in range(count):
        gate_copies[d].start()

    len_copy.wait()
    row_copy.wait()
    token = me * tokens + lax.broadcasted_iota(jnp.int32, (8, tokens), 1)
    mine = me * owned + lax.broadcasted_iota(jnp.int32, (owned, LANES), 0)
    start = jnp.int32(0)
    token_row = jnp.zeros((8, tokens), jnp.int32)
    sizes = jnp.zeros((owned, LANES), jnp.int32)
    for k in range(segs):
        stop = start + lengths[k]
        token_row = jnp.where((token >= start) & (token < stop), rows[k], token_row)
        sizes = jnp.where(mine == rows[k], lengths[k], sizes)
        start = stop
    row_at = lax.broadcasted_iota(jnp.int32, (segs, tokens), 0)
    member[...] = (row_at == token_row[0:1, :]).astype(jnp.float32).astype(jnp.bfloat16)

    fwd_copy.wait()

    def to_spectrum(source, index, spec):
        high, low = split_value(source[...])
        both = mul(fwd_v[0], jnp.concatenate([high, low], axis=1))
        spec[index] = both[:, :lanes] + (both[:, lanes:] + mul(fwd_v[1], high))

    sig_copies[0].wait()
    for h in range(halves):
        to_spectrum(sig_own.at[0, pieces[h], :], me * halves + h, spec_s)
    tap_copy.wait()
    for h in range(halves):
        to_spectrum(tap_in.at[0, pieces[h], :], me * halves + h, spec_h)
    for h in range(halves):
        for e in range(count - 1):
            sig_sends[e, h].wait_recv()
            if h + 1 < halves:
                tap_sends[e, h + 1].start()
        for d in order:
            to_spectrum(sig_in.at[d, pieces[h], :], peers[d] * halves + h, spec_s)

    def take_taps(h):
        for e, d in enumerate(order):
            tap_sends[e, h].wait_recv()
            to_spectrum(tap_in.at[d, pieces[h], :], peers[d] * halves + h, spec_h)

    def load(spec, wanted, re, im):
        return {i: (spec[i, re, :], spec[i, im, :]) for i in wanted}

    def products(first, last, lags, final):
        def tile(sign, row):
            re = pl.ds(pl.multiple_of(row, 8), 8)
            im = pl.ds(pl.multiple_of(row + block, 8), 8)
            used = [k for k in lags if k < last]
            taps_at = load(spec_h, used, re, im)
            sig_at = load(spec_s, sorted({j - k for j in range(first, last) for k in used if k <= j}), re, im)
            old = (acc[first - 1, re, :], acc[first - 1, im, :]) if final and first else None
            for j in range(first, last):
                total = (acc[j, re, :], acc[j, im, :]) if final else None
                for k in used:
                    if k <= j:
                        (a, b), (c, d) = sig_at[j - k], taps_at[k]
                        new = (a * c - b * d, a * d + b * c)
                        total = new if total is None else (total[0] + new[0], total[1] + new[1])
                if not final:
                    acc[j, re, :], acc[j, im, :] = total
                    continue
                out = total
                if j:
                    out = (total[0] - sign * old[1], total[1] + sign * old[0])
                at = pl.ds((j % halves) * lanes, lanes)
                prod[j // halves, re, at], prod[j // halves, im, at] = out
                old = total
            if final and last < blocks:
                acc[last - 1, re, :], acc[last - 1, im, :] = old

        for sign, base in ((1, 0), (-1, block // 2)):
            def body(t, state, sign=sign, base=base):
                tile(sign, base + t * 8)
                return state
            lax.fori_loop(0, block // 16, body, 0)

    for h in range(halves - 1):
        take_taps(h)
    products(0, blocks, [k for k in range(blocks) if k % halves < halves - 1], False)
    take_taps(halves - 1)
    late_lags = [k for k in range(blocks) if k % halves == halves - 1]

    def back_copy(d, h, peer):
        return remote(
            conv_out.at[d, pieces[h], :], conv_in.at[d, pieces[h], :], send_c.at[d, h], recv_c.at[d, h], peer
        )

    def give_back(d):
        high, low = split_value(prod[peers[d]])
        result = mul(inv_v[0], high) + (mul(inv_v[1], high) + mul(inv_v[0], low))
        for h in range(halves):
            conv_out[d, pieces[h], :] = result[:, h * lanes:(h + 1) * lanes]

    inv_copy.wait()
    products(0, blocks, late_lags, True)
    for d in order:
        give_back(d)
        for h in range(halves):
            back_copy(d, h, peers[d]).start()
    give_back(0)

    out_copies = []

    def finish(d, h, conv):
        at = cols(peers[d])
        value = gate_own[d, pieces[h], :] * (conv[d, pieces[h], :] + skip[:, at] * sig_own[d, pieces[h], :])
        mixed_v[d, pieces[h], :] = value
        copy = pltpu.make_async_copy(mixed_v.at[d, pieces[h], :], mixed.at[pieces[h], at], out_sem.at[d, h])
        copy.start()
        out_copies.append(copy)
        high, low = split_value(value)
        inside = member[:, h * block:(h + 1) * block]
        sums = mul(inside, high) + mul(inside, low)
        for p in range(count):
            new = sums[p * owned:(p + 1) * owned]
            part[p, :, at] = part[p, :, at] + new if h else new

    skip_copy.wait()
    for d in range(count):
        if d:
            sig_copies[d].wait()
        gate_copies[d].wait()
    for h in range(halves):
        finish(0, h, conv_out)
    for d in order:
        for h in range(halves):
            back_copy(d, h, peers[d]).wait_recv()
            finish(d, h, conv_in)

    part_sends = [
        remote(part.at[peers[d]], part_in.at[d], send_p.at[d], recv_p.at[d], peers[d]) for d in order
    ]
    for copy in part_sends:
        copy.start()
    total = part[me]
    for d, copy in zip(order, part_sends):
        copy.wait_recv()
        total = total + part_in[d]
    pooled[...] = total / jnp.concatenate([sizes] * (width // LANES), axis=1).astype(jnp.float32)

    for copy in out_copies:
        copy.wait()
    for copy in [*sig_sends.values(), *tap_sends.values(), *part_sends]:
        copy.wait_send()
    for d in order:
        for h in range(halves):
            back_copy(d, h, peers[d]).wait_send()


def store_kernel(mixed_v, pooled_v, mixed, pooled, sem):
    rows = mixed.shape[0] // STORES
    parts = [pl.ds(i * rows, rows) for i in range(STORES)]
    copies = [pltpu.make_async_copy(mixed_v.at[at, :], mixed.at[at, :], sem.at[i]) for i, at in enumerate(parts)]
    copies.append(pltpu.make_async_copy(pooled_v, pooled, sem.at[STORES]))
    for copy in copies:
        copy.start()
    for copy in copies:
        copy.wait()


def fits_kernel(tokens, width, count):
    return (
        count > 1
        and count & (count - 1) == 0
        and width % (count * LANES) == 0
        and tokens % (4 * LANES) == 0
    )


def fused_on_device(count, signal, filter_taps, out_gate, skip_gain, lengths, row_of_segment):
    tokens, width = signal.shape
    lanes = width // count
    block = 2 * LANES
    halves = tokens // block
    owned = lengths.shape[0] // count
    segs = owned * count
    forward, inverse = transform_tables(block)
    f32, bf16 = jnp.float32, jnp.bfloat16
    dma = pltpu.SemaphoreType.DMA
    each = dma((count, halves))
    anywhere = pl.BlockSpec(memory_space=pl.ANY)
    vmem = pl.BlockSpec(memory_space=pltpu.VMEM)
    piece = pltpu.VMEM((count, tokens, lanes), f32)
    spectra = pltpu.VMEM((count * halves, 2 * block, lanes), f32)
    results = pl.pallas_call(
        functools.partial(mixer_kernel, count, block),
        out_shape=(
            pltpu.VMEM((tokens, width), f32),
            pltpu.VMEM((owned, width), f32),
        ),
        in_specs=[anywhere] * 8,
        out_specs=(anywhere, vmem),
        scratch_shapes=[
            piece, piece, piece, piece, spectra, spectra,
            pltpu.VMEM((count, 2 * block, halves * lanes), f32),
            spectra,
            piece, piece, piece,
            pltpu.VMEM((segs, tokens), bf16),
            pltpu.VMEM((count, owned, width), f32),
            pltpu.VMEM((count, owned, width), f32),
            pltpu.VMEM(forward.shape, bf16),
            pltpu.VMEM(inverse.shape, bf16),
            pltpu.SMEM(lengths.shape, jnp.int32),
            pltpu.SMEM(lengths.shape, jnp.int32),
            pltpu.VMEM((1, width), f32),
            dma((count,)), dma((5,)), dma((count,)), dma,
            each, each, each, each, each, each,
            dma((count,)), dma((count,)), each,
        ],
        compiler_params=pltpu.CompilerParams(
            collective_id=0, has_side_effects=True, vmem_limit_bytes=62 * 1024 * 1024
        ),
        name="mixer",
    )(
        lengths, row_of_segment, signal, filter_taps, out_gate, skip_gain[None, :],
        jnp.asarray(forward), jnp.asarray(inverse),
    )
    return pl.pallas_call(
        store_kernel,
        out_shape=tuple(pltpu.HBM(result.shape, f32) for result in results),
        in_specs=[anywhere] * 2,
        out_specs=(anywhere,) * 2,
        scratch_shapes=[dma((STORES + 1,))],
        compiler_params=pltpu.CompilerParams(vmem_limit_bytes=1024 * 1024),
        name="store",
    )(*results)


def on_device(signal, filter_taps, out_gate, skip_gain, lengths, row_of_segment):
    seq_count = lax.axis_size("seq")
    if fits_kernel(signal.shape[0], signal.shape[1], seq_count):
        return fused_on_device(
            seq_count, signal, filter_taps, out_gate, skip_gain, lengths, row_of_segment
        )
    seq_index = lax.axis_index("seq")
    conv = convolve_channels(signal, filter_taps)
    mixed = out_gate * (conv + skip_gain[None, :] * signal)
    pooled = pool_segments(mixed, lengths, row_of_segment, seq_index, seq_count)
    return (mixed, pooled)


def solution(mesh):
    placed = (P("seq", "chan"), P("seq", "chan"), P("seq", "chan"), P("chan"), P(), P())
    return jax.shard_map(
        on_device,
        mesh=mesh,
        in_specs=placed,
        out_specs=(P("seq", "chan"), P("seq", "chan")),
        check_vma=False,
    )
```
